256 devices in a mesh: row: 8 (over x, core), col: 32 (over z, y).
Axes of the slice: x: 4, y: 4, z: 8, core: 2. Of those that a mesh axis runs over, the one named last changes fastest.
Arguments:
- tokens: bfloat16 [1024, 8192], P('col', 'row'), may hold values from -6 to 6
- gate_weight: bfloat16 [8192, 24576], P('row', 'col'), may hold values from -0.0625 to 0.0625
- up_weight: bfloat16 [8192, 24576], P('row', 'col'), may hold values from -0.0625 to 0.0625
- down_weight: bfloat16 [24576, 8192], P('col', 'row'), may hold values from -0.0390625 to 0.0390625
- out_grad: bfloat16 [1024, 8192], P('col', 'row'), may hold values from -6 to 6
Outputs:
- mixed: bfloat16 [1024, 8192], P('col', 'row')
- input_grad: bfloat16 [1024, 8192], P('col', 'row')
- gate_grad: bfloat16 [8192, 24576], P('row', 'col')
- up_grad: bfloat16 [8192, 24576], P('row', 'col')
- down_grad: bfloat16 [24576, 8192], P('col', 'row')
The draws below stay inside these ranges and needn't reach their ends.
All inputs are finite; a program needn't handle non-finite values.
Results may differ from the reference program's by a relative error of at most 0.034.
Values may be sent and summed in bfloat16 or wider, within the bound.
No kernel may reach another device: no remote copies, remote signals or barrier semaphores. Data moves between devices by JAX's collectives and lax.ppermute only.
A program may use at most 128 MiB of HBM per device.

```python
import jax
import jax.numpy as jnp
from jax import lax

D = 8192
FF = 24576
TOKENS = 1024
N_ROW = 8
N_COL = 32


def block_levels(own_key, shape, shards, least, top_value):
    level = 1.0
    for dim, blocks in shards:
        draws = jax.random.uniform(jax.random.fold_in(jax.random.fold_in(own_key, 6), dim), (blocks,), jnp.float32, least / len(shards), top_value / len(shards))
        level = level * jnp.repeat(jnp.exp(draws), shape[dim] // blocks).reshape((-1,) + (1,) * (len(shape) - 1 - dim))
    return level


def normal_values(stream_key, dims, scale, reach, pieces=(), held_as=jnp.bfloat16):
    values = jax.random.normal(stream_key, dims, jnp.float32) * scale
    if len(pieces) > 0:
        values = block_levels(stream_key, dims, pieces, -0.22, 0.18) * values
    return jnp.clip(values, min=-reach, max=reach).astype(held_as)


def setup_inputs(seed: int = 0) -> dict:
    seeds = jax.random.split(jax.random.key(seed), 6)
    return {
        "tokens": normal_values(seeds[0], (TOKENS, D), 1.0, 6.0, ((0, 32), (1, 8))),
        "gate_weight": normal_values(seeds[1], (D, FF), D ** -0.5, 0.0625, ((0, 8), (1, 32))),
        "up_weight": normal_values(seeds[2], (D, FF), D ** -0.5, 0.0625, ((0, 8), (1, 32))),
        "down_weight": normal_values(seeds[3], (FF, D), FF ** -0.5, 0.0390625, ((0, 32), (1, 8))),
        "out_grad": normal_values(seeds[4], (TOKENS, D), 0.5, 6.0, ((0, 32), (1, 8))),
    }


def block_terms(left, right, count):
    width = left.shape[1] // count

    def step(total, index):
        start = (index * width).astype(jnp.int32)
        left_part = lax.dynamic_slice_in_dim(left, start, width, 1)
        right_part = lax.dynamic_slice_in_dim(right, start, width, 0)
        term = jnp.dot(left_part, right_part, preferred_element_type=jnp.float32)
        rounded = lax.optimization_barrier(term.astype(jnp.bfloat16))
        return total + rounded.astype(jnp.float32), None

    empty = jnp.zeros((left.shape[0], right.shape[1]), jnp.float32)
    total, unused = lax.scan(step, empty, jnp.arange(count, dtype=jnp.int32))
    return total


def block_pairs(left_one, right_one, left_two, right_two, count):
    width = left_one.shape[1] // count

    def step(total, index):
        start = (index * width).astype(jnp.int32)
        first = jnp.dot(lax.dynamic_slice_in_dim(left_one, start, width, 1), lax.dynamic_slice_in_dim(right_one, start, width, 0), preferred_element_type=jnp.float32)
        second = jnp.dot(lax.dynamic_slice_in_dim(left_two, start, width, 1), lax.dynamic_slice_in_dim(right_two, start, width, 0), preferred_element_type=jnp.float32)
        rounded = lax.optimization_barrier((first + second).astype(jnp.bfloat16))
        return total + rounded.astype(jnp.float32), None

    empty = jnp.zeros((left_one.shape[0], right_one.shape[1]), jnp.float32)
    total, unused = lax.scan(step, empty, jnp.arange(count, dtype=jnp.int32))
    return total


def reference(tokens, gate_weight, up_weight, down_weight, out_grad):
    gate = block_terms(tokens, gate_weight, N_ROW)
    up = block_terms(tokens, up_weight, N_ROW)
    sig = jax.nn.sigmoid(gate)
    hidden = (gate * sig * up).astype(jnp.bfloat16)
    mixed = block_terms(hidden, down_weight, N_COL).astype(jnp.bfloat16)
    down_grad = jnp.dot(hidden.T, out_grad, preferred_element_type=jnp.float32).astype(jnp.bfloat16)
    hidden_grad = block_terms(out_grad, down_weight.T, N_ROW)
    pre_gate = (hidden_grad * up * sig * (1.0 + gate * (1.0 - sig))).astype(jnp.bfloat16)
    pre_up = (hidden_grad * gate * sig).astype(jnp.bfloat16)
    gate_grad = jnp.dot(tokens.T, pre_gate, preferred_element_type=jnp.float32).astype(jnp.bfloat16)
    up_grad = jnp.dot(tokens.T, pre_up, preferred_element_type=jnp.float32).astype(jnp.bfloat16)
    input_sum = block_pairs(pre_gate, gate_weight.T, pre_up, up_weight.T, N_COL)
    input_grad = input_sum.astype(jnp.bfloat16)
    return mixed, input_grad, gate_grad, up_grad, down_grad
```

```python
import jax
import jax.numpy as jnp
from jax import lax
from jax.sharding import PartitionSpec as P

BF16 = jnp.bfloat16
F32 = jnp.float32
NX, NC, NZ, NY = 4, 2, 8, 4

X_GROUPS = [[x * NC + c for x in range(NX)] for c in range(NC)]
Y_GROUPS = [[z * NY + y for y in range(NY)] for z in range(NZ)]
Z_GROUPS = [[z * NY + y for z in range(NZ)] for y in range(NY)]
CORE_PAIRS = [(r, r ^ 1) for r in range(NX * NC)]


def swap_core(value):
    return lax.ppermute(value, "row", CORE_PAIRS)


def exchange(value, axis, groups):
    return lax.all_to_all(value, axis, 0, 0, axis_index_groups=groups, tiled=True)


def share(value, axis, groups):
    return exchange(jnp.tile(value, (len(groups[0]), 1)), axis, groups)


def scatter_sum(value, axis, groups):
    count = len(groups[0])
    got = exchange(value, axis, groups)
    return got.reshape(count, value.shape[0] // count, value.shape[1]).astype(F32).sum(0)


def dot(left, right):
    return jnp.dot(left, right, preferred_element_type=F32)


def dot_rows(left, right):
    return lax.dot_general(left, right, (((0,), (0,)), ((), ())), preferred_element_type=F32)


def dot_cols(left, right):
    return lax.dot_general(left, right, (((1,), (1,)), ((), ())), preferred_element_type=F32)


def after(value, *others):
    return lax.optimization_barrier((value,) + others)[0]


def body(tokens, gate_weight, up_weight, down_weight, out_grad):
    core = lax.axis_index("row") % NC
    half = tokens.shape[0] // NC

    def halves(value):
        mine = lax.dynamic_slice_in_dim(value, core * half, half, 0)
        other = lax.dynamic_slice_in_dim(value, (1 - core) * half, half, 0)
        return jnp.concatenate([mine, swap_core(other)], axis=1)

    def join(value):
        width = value.shape[1] // 2
        mine = value[:, :width]
        got = swap_core(value[:, width:])
        first = jnp.where(core == 0, mine, got)
        second = jnp.where(core == 0, got, mine)
        return jnp.concatenate([first, second], axis=0)

    width = tokens.shape[1]
    hidden_width = gate_weight.shape[1]

    tok = halves(tokens)
    grad = halves(out_grad)
    gate_up = jnp.concatenate([gate_weight, up_weight], axis=1)
    gate_up = jnp.concatenate([gate_up, swap_core(gate_up)], axis=0)
    down = jnp.concatenate([down_weight, swap_core(down_weight)], axis=1)

    tok_z = share(tok, "col", Z_GROUPS)
    grad_z = lax.all_gather(grad, "col", axis=0, axis_index_groups=Z_GROUPS, tiled=True)
    tok_all = share(tok_z, "col", Y_GROUPS)
    grad_all = share(after(grad_z, tok_all), "col", Y_GROUPS)

    gate_up_sum = scatter_sum(dot(tok_all, gate_up).astype(BF16), "row", X_GROUPS)
    gate, up = gate_up_sum[:, :hidden_width], gate_up_sum[:, hidden_width:]
    hidden_grad = scatter_sum(dot_cols(grad_all, down).astype(BF16), "row", X_GROUPS)

    sig = jax.nn.sigmoid(gate)
    hidden_own = (gate * sig * up).astype(BF16)
    pre_gate_own = (hidden_grad * up * sig * (1.0 + gate * (1.0 - sig))).astype(BF16)
    pre_up_own = (hidden_grad * gate * sig).astype(BF16)

    def gather_x(value):
        return lax.all_gather(value, "row", axis=0, axis_index_groups=X_GROUPS, tiled=True)

    hidden = gather_x(hidden_own)
    pre_gate = gather_x(pre_gate_own)
    pre_up = gather_x(pre_up_own)

    mixed_y = scatter_sum(dot(hidden, down).astype(BF16), "col", Y_GROUPS)
    pre = jnp.concatenate([pre_gate, pre_up], axis=1)
    input_y = scatter_sum(dot_cols(pre, gate_up).astype(BF16), "col", Y_GROUPS)
    both = jnp.concatenate([mixed_y.astype(BF16), input_y.astype(BF16)], axis=1)
    both = scatter_sum(both, "col", Z_GROUPS).astype(BF16)
    mixed = join(both[:, : 2 * width])
    input_grad = join(both[:, 2 * width :])

    def all_tokens(value):
        return jnp.concatenate([value, swap_core(value)], axis=0)

    def all_rows(value):
        return jnp.concatenate([value[:, :width], swap_core(value[:, width:])], axis=0)

    tok_rows = all_rows(tok_all)
    grad_rows = all_rows(grad_all)
    down_grad = dot_rows(all_tokens(hidden), grad_rows).astype(BF16)
    gate_grad = dot_rows(tok_rows, all_tokens(pre_gate)).astype(BF16)
    up_grad = dot_rows(tok_rows, all_tokens(pre_up)).astype(BF16)
    return (mixed, input_grad, gate_grad, up_grad, down_grad)


def solution(mesh):
    in_specs = (P("col", "row"), P("row", "col"), P("row", "col"), P("col", "row"), P("col", "row"))
    out_specs = (
        P("col", "row"),
        P("col", "row"),
        P("row", "col"),
        P("row", "col"),
        P("col", "row"),
    )
    return jax.shard_map(body, mesh=mesh, in_specs=in_specs, out_specs=out_specs, check_vma=False)
```

```python
import jax
import jax.numpy as jnp
from jax import lax
from jax.experimental import pallas as pl
from jax.experimental.pallas import tpu as pltpu
from jax.sharding import PartitionSpec as P

BF16 = jnp.bfloat16
F32 = jnp.float32
NX, NC, NZ, NY = 4, 2, 8, 4
MIB = 1024 * 1024

X_GROUPS = [[x * NC + c for x in range(NX)] for c in range(NC)]
Y_GROUPS = [[z * NY + y for y in range(NY)] for z in range(NZ)]
Z_GROUPS = [[z * NY + y for z in range(NZ)] for y in range(NY)]
Y_UP = [(z * NY + y, z * NY + (y + 1) % NY) for z in range(NZ) for y in range(NY)]
Y_DOWN = [(dst, src) for src, dst in Y_UP]
X_UP = [(x * NC + c, (x + 1) % NX * NC + c) for x in range(NX) for c in range(NC)]
X_DOWN = [(dst, src) for src, dst in X_UP]
CORE_PAIRS = [(r, r ^ 1) for r in range(NX * NC)]

NN = (((1,), (0,)), ((), ()))
NT = (((1,), (1,)), ((), ()))
TN = (((0,), (0,)), ((), ()))


def dot(left, right, dims):
    return lax.dot_general(left, right, dims, preferred_element_type=F32)


def swap_core(value):
    return lax.ppermute(value, "row", CORE_PAIRS)


def exchange(value, axis, groups):
    count = len(groups[0])
    got = lax.all_to_all(value, axis, 0, 0, axis_index_groups=groups, tiled=True)
    return got.reshape(count, value.shape[0] // count, value.shape[1])


def share(value, axis, groups):
    got = exchange(jnp.tile(value, (len(groups[0]), 1)), axis, groups)
    return got.reshape(-1, value.shape[1])


def after(value, *others):
    return lax.optimization_barrier((value,) + others)[0]


def ring_blocks(own, axis, up, down):
    half = own.shape[0] // 2
    before = lax.ppermute(own, axis, up)
    behind = lax.ppermute(own, axis, down)
    top = lax.ppermute(before[:half], axis, up)
    bottom = lax.ppermute(behind[half:], axis, down)
    return own, behind, top, bottom, before


def whole(shape):
    return pl.BlockSpec(shape, lambda *_: (0,) * len(shape))


def call(kernel, grid, in_specs, out_specs, out_shape, flops, scratch=(), limit=24):
    return pl.pallas_call(
        kernel,
        grid_spec=pltpu.PrefetchScalarGridSpec(
            num_scalar_prefetch=1,
            grid=grid,
            in_specs=in_specs,
            out_specs=out_specs,
            scratch_shapes=list(scratch),
        ),
        out_shape=out_shape,
        compiler_params=pltpu.CompilerParams(vmem_limit_bytes=limit * MIB),
        cost_estimate=pl.CostEstimate(flops=flops, bytes_accessed=10 * MIB, transcendentals=0),
    )


def place(index, own, behind, top, bottom, before, store):
    rows = own.shape[0]
    half = rows // 2
    store(lax.rem(index, 4), 0, own)
    store(lax.rem(index + 1, 4), 0, behind)
    store(lax.rem(index + 2, 4), 0, top)
    store(lax.rem(index + 2, 4), half, bottom)
    store(lax.rem(index + 3, 4), 0, before)


def gate_up_kernel(index, tok, gate_a, gate_b, up_a, up_b, out):
    del index
    step = pl.program_id(0)
    width = gate_a.shape[0]

    def part(one, two):
        total = dot(tok[:, :width], one[...], NN) + dot(tok[:, width:], two[...], NN)
        out[...] = total.astype(BF16)

    @pl.when(step < pl.num_programs(0) // 2)
    def _():
        part(gate_a, gate_b)

    @pl.when(step >= pl.num_programs(0) // 2)
    def _():
        part(up_a, up_b)


def gate_up_product(index, tok, gate_a, gate_b, up_a, up_b):
    rows, depth = tok.shape
    width, cols = gate_a.shape
    tile = 256
    steps = cols // tile
    first = pl.BlockSpec((width, tile), lambda j, _: (0, jnp.minimum(j, steps - 1)))
    second = pl.BlockSpec((width, tile), lambda j, _: (0, jnp.maximum(j - steps, 0)))
    return call(
        gate_up_kernel,
        (2 * steps,),
        [whole(tok.shape), first, first, second, second],
        pl.BlockSpec((rows, tile), lambda j, _: (0, j)),
        jax.ShapeDtypeStruct((rows, 2 * cols), BF16),
        4 * rows * depth * cols,
    )(index, tok, gate_a, gate_b, up_a, up_b)


def hidden_term_kernel(index, own, behind, top, bottom, before, down_a, down_b, out, mine, other):
    step = pl.program_id(0)
    rows = own.shape[0]
    width = own.shape[1] // 2

    @pl.when(step == 0)
    def _():
        def store(block, first, value):
            start = pl.multiple_of(block * rows + first, rows // 2)
            mine[pl.ds(start, value.shape[0]), :] = value[:, :width]
            other[pl.ds(start, value.shape[0]), :] = value[:, width:]

        place(index[0], own, behind, top, bottom, before, store)

    total = dot(mine[...], down_a[...], NT) + dot(other[...], down_b[...], NT)
    out[...] = total.astype(BF16)


def hidden_term_product(index, blocks, down_a, down_b):
    rows, depth = blocks[0].shape
    cols, width = down_a.shape
    tile = 256
    weight = pl.BlockSpec((tile, width), lambda j, _: (j, 0))
    half = jax.ShapeDtypeStruct((4 * rows, width), BF16)
    return call(
        hidden_term_kernel,
        (cols // tile,),
        [whole(block.shape) for block in blocks] + [weight, weight],
        [pl.BlockSpec((4 * rows, tile), lambda j, _: (0, j)), whole(half.shape), whole(half.shape)],
        [jax.ShapeDtypeStruct((4 * rows, cols), BF16), half, half],
        8 * rows * depth * cols,
    )(index, *blocks, down_a, down_b)


def mixed_kernel(index, own, behind, top, bottom, before, down_a, down_b, out, hidden):
    step = pl.program_id(0)
    rows = own.shape[0]

    @pl.when(step == 0)
    def _():
        def store(block, first, value):
            start = pl.multiple_of(block * rows + first, rows // 2)
            hidden[pl.ds(start, value.shape[0]), :] = value[...]

        place(index[0], own, behind, top, bottom, before, store)

    @pl.when(step < pl.num_programs(0) // 2)
    def _():
        out[...] = dot(hidden[...], down_a[...], NN).astype(BF16)

    @pl.when(step >= pl.num_programs(0) // 2)
    def _():
        out[...] = dot(hidden[...], down_b[...], NN).astype(BF16)


def mixed_product(index, blocks, down_a, down_b):
    rows, depth = blocks[0].shape
    width = down_a.shape[1]
    tile = 512
    steps = width // tile
    shape = (4 * rows, depth)
    return call(
        mixed_kernel,
        (2 * steps,),
        [whole(block.shape) for block in blocks]
        + [
            pl.BlockSpec((depth, tile), lambda j, _: (0, jnp.minimum(j, steps - 1))),
            pl.BlockSpec((depth, tile), lambda j, _: (0, jnp.maximum(j - steps, 0))),
        ],
        [pl.BlockSpec((4 * rows, tile), lambda j, _: (0, j)), whole(shape)],
        [jax.ShapeDtypeStruct((4 * rows, 2 * width), BF16), jax.ShapeDtypeStruct(shape, BF16)],
        16 * rows * depth * width,
    )(index, *blocks, down_a, down_b)


def input_kernel(
    index, own, behind, top, bottom, before, gate_a, up_a, gate_b, up_b, out, pre_gate, pre_up
):
    step = pl.program_id(0)
    rows = own.shape[0]
    cols = own.shape[1] // 2

    @pl.when(step == 0)
    def _():
        def store(block, first, value):
            start = pl.multiple_of(block * rows + first, rows // 2)
            pre_gate[pl.ds(start, value.shape[0]), :] = value[:, :cols]
            pre_up[pl.ds(start, value.shape[0]), :] = value[:, cols:]

        place(index[0], own, behind, top, bottom, before, store)

    def part(gate, up):
        total = dot(pre_gate[...], gate[...], NT) + dot(pre_up[...], up[...], NT)
        out[...] = total.astype(BF16)

    @pl.when(step < pl.num_programs(0) // 2)
    def _():
        part(gate_a, up_a)

    @pl.when(step >= pl.num_programs(0) // 2)
    def _():
        part(gate_b, up_b)


def input_product(index, blocks, gate_a, up_a, gate_b, up_b):
    rows = blocks[0].shape[0]
    width, cols = gate_a.shape
    tile = 256
    steps = width // tile
    first = pl.BlockSpec((tile, cols), lambda j, _: (jnp.minimum(j, steps - 1), 0))
    second = pl.BlockSpec((tile, cols), lambda j, _: (jnp.maximum(j - steps, 0), 0))
    half = jax.ShapeDtypeStruct((4 * rows, cols), BF16)
    return call(
        input_kernel,
        (2 * steps,),
        [whole(block.shape) for block in blocks] + [first, first, second, second],
        [pl.BlockSpec((4 * rows, tile), lambda j, _: (0, j)), whole(half.shape), whole(half.shape)],
        [jax.ShapeDtypeStruct((4 * rows, 2 * width), BF16), half, half],
        32 * rows * cols * width,
    )(index, *blocks, gate_a, up_a, gate_b, up_b)


def total_of(terms):
    total = terms[0].astype(F32)
    for k in range(1, terms.shape[0]):
        total = total + terms[k].astype(F32)
    return total


def hidden_kernel(index, terms, gate_up, hidden):
    del index
    total = total_of(terms)
    cols = hidden.shape[1]
    gate, up = total[:, :cols], total[:, cols:]
    gate_up[...] = total
    hidden[...] = (gate * jax.nn.sigmoid(gate) * up).astype(BF16)


def hidden_of(index, terms):
    _, rows, cols = terms.shape
    return call(
        hidden_kernel,
        (1,),
        [whole(terms.shape)],
        [whole((rows, cols)), whole((rows, cols // 2))],
        [
            jax.ShapeDtypeStruct((rows, cols), F32),
            jax.ShapeDtypeStruct((rows, cols // 2), BF16),
        ],
        16 * rows * cols,
    )(index, terms)


def pre_kernel(index, terms, gate_up, out):
    del index
    hidden_grad = total_of(terms)
    cols = hidden_grad.shape[1]
    gate, up = gate_up[:, :cols], gate_up[:, cols:]
    sig = jax.nn.sigmoid(gate)
    out[:, :cols] = (hidden_grad * up * sig * (1.0 + gate * (1.0 - sig))).astype(BF16)
    out[:, cols:] = (hidden_grad * gate * sig).astype(BF16)


def pre_grads(index, terms, gate_up):
    return call(
        pre_kernel,
        (1,),
        [whole(terms.shape), whole(gate_up.shape)],
        whole(gate_up.shape),
        jax.ShapeDtypeStruct(gate_up.shape, BF16),
        16 * gate_up.size,
    )(index, terms, gate_up)


def sums_kernel(index, one, two, out):
    del index
    cols = one.shape[2]
    out[:, :cols] = total_of(one).astype(BF16)
    out[:, cols:] = total_of(two).astype(BF16)


def sums_of(index, one, two):
    _, rows, cols = one.shape
    return call(
        sums_kernel,
        (1,),
        [whole(one.shape), whole(two.shape)],
        whole((rows, 2 * cols)),
        jax.ShapeDtypeStruct((rows, 2 * cols), BF16),
        16 * rows * cols,
    )(index, one, two)


def body(tokens, gate_weight, up_weight, down_weight, out_grad):
    core = lax.axis_index("row") % NC
    x = (lax.axis_index("row") // NC).astype(jnp.int32).reshape(1)
    y = (lax.axis_index("col") % NY).astype(jnp.int32).reshape(1)
    half = tokens.shape[0] // NC
    width = tokens.shape[1]

    def halves(value):
        mine = lax.dynamic_slice_in_dim(value, core * half, half, 0)
        other = lax.dynamic_slice_in_dim(value, (1 - core) * half, half, 0)
        return jnp.concatenate([mine, swap_core(other)], axis=1)

    def join(value):
        mine = value[:, :width]
        got = swap_core(value[:, width:])
        first = jnp.where(core == 0, mine, got)
        second = jnp.where(core == 0, got, mine)
        return jnp.concatenate([first, second], axis=0)

    both = jnp.concatenate([halves(tokens), halves(out_grad)], axis=1)
    gate_other = swap_core(gate_weight)
    up_other = swap_core(up_weight)
    down_other = swap_core(down_weight)

    both_z = share(both, "col", Z_GROUPS)
    tok = share(both_z[:, : 2 * width], "col", Y_GROUPS)
    grad_z = after(both_z[:, 2 * width :], tok)
    grad_blocks = ring_blocks(grad_z, "col", Y_UP, Y_DOWN)

    gate_up_term = gate_up_product(y, tok, gate_weight, gate_other, up_weight, up_other)
    gate_up, hidden_own = hidden_of(y, exchange(gate_up_term, "row", X_GROUPS))
    hidden_term, grad_mine, grad_other = hidden_term_product(y, grad_blocks, down_weight, down_other)
    pre_own = pre_grads(y, exchange(hidden_term, "row", X_GROUPS), gate_up)

    hidden_blocks = ring_blocks(hidden_own, "row", X_UP, X_DOWN)
    mixed_term, hidden = mixed_product(x, hidden_blocks, down_weight, down_other)
    pre_blocks = ring_blocks(pre_own, "row", X_UP, X_DOWN)
    input_term, pre_gate, pre_up = input_product(
        x, pre_blocks, gate_weight, up_weight, gate_other, up_other
    )
    mixed_y = exchange(mixed_term, "col", Y_GROUPS)
    input_y = exchange(input_term, "col", Y_GROUPS)
    sums = exchange(sums_of(y, mixed_y, input_y), "col", Z_GROUPS).astype(F32).sum(0).astype(BF16)
    mixed = join(sums[:, : 2 * width])
    input_grad = join(sums[:, 2 * width :])

    def all_tokens(value):
        return jnp.concatenate([value, swap_core(value)], axis=0)

    tok_rows = jnp.concatenate([tok[:, :width], swap_core(tok[:, width:])], axis=0)
    grad_rows = jnp.concatenate([grad_mine, swap_core(grad_other)], axis=0)
    down_grad = dot(all_tokens(hidden), grad_rows, TN).astype(BF16)
    gate_grad = dot(tok_rows, all_tokens(pre_gate), TN).astype(BF16)
    up_grad = dot(tok_rows, all_tokens(pre_up), TN).astype(BF16)
    return (mixed, input_grad, gate_grad, up_grad, down_grad)


def solution(mesh):
    in_specs = (P("col", "row"), P("row", "col"), P("row", "col"), P("col", "row"), P("col", "row"))
    out_specs = (
        P("col", "row"),
        P("col", "row"),
        P("row", "col"),
        P("row", "col"),
        P("col", "row"),
    )
    return jax.shard_map(body, mesh=mesh, in_specs=in_specs, out_specs=out_specs, check_vma=False)
```

```python
import jax
import jax.numpy as jnp
from jax import lax
from jax.experimental import pallas as pl
from jax.experimental.pallas import tpu as pltpu
from jax.sharding import PartitionSpec as P

BF16 = jnp.bfloat16
F32 = jnp.float32
NX, NC, NZ, NY = 4, 2, 8, 4
MIB = 1024 * 1024

X_GROUPS = [[x * NC + c for x in range(NX)] for c in range(NC)]
Y_GROUPS = [[z * NY + y for y in range(NY)] for z in range(NZ)]
Z_GROUPS = [[z * NY + y for z in range(NZ)] for y in range(NY)]
Z_UP = [(z * NY + y, (z + 1) % NZ * NY + y) for z in range(NZ) for y in range(NY)]
Z_DOWN = [(dst, src) for src, dst in Z_UP]
X_UP = [(x * NC + c, (x + 1) % NX * NC + c) for x in range(NX) for c in range(NC)]
X_DOWN = [(dst, src) for src, dst in X_UP]
CORE_PAIRS = [(r, r ^ 1) for r in range(NX * NC)]

NN = (((1,), (0,)), ((), ()))
NT = (((1,), (1,)), ((), ()))
TN = (((0,), (0,)), ((), ()))


def dot(left, right, dims):
    return lax.dot_general(left, right, dims, preferred_element_type=F32)


def swap_core(value):
    return lax.ppermute(value, "row", CORE_PAIRS)


def exchange(value, axis, groups):
    count = len(groups[0])
    got = lax.all_to_all(value, axis, 0, 0, axis_index_groups=groups, tiled=True)
    return got.reshape(count, value.shape[0] // count, value.shape[1])


def share(value, axis, groups):
    got = exchange(jnp.tile(value, (len(groups[0]), 1)), axis, groups)
    return got.reshape(-1, value.shape[1])


def after(value, *others):
    return lax.optimization_barrier((value,) + others)[0]


def ring_blocks(own, axis, up, down):
    half = own.shape[0] // 2
    before = lax.ppermute(own, axis, up)
    behind = lax.ppermute(own, axis, down)
    top = lax.ppermute(before[:half], axis, up)
    bottom = lax.ppermute(behind[half:], axis, down)
    return own, behind, top, bottom, before


def ring_eight(own, axis, up, down):
    half = own.shape[0] // 2
    before, behind = [own], [own]
    for _ in range(3):
        before.append(lax.ppermute(before[-1], axis, up))
        behind.append(lax.ppermute(behind[-1], axis, down))
    top = lax.ppermute(before[3][:half], axis, up)
    bottom = lax.ppermute(behind[3][half:], axis, down)
    return own, behind[1], behind[2], behind[3], top, bottom, before[3], before[2], before[1]


def whole(shape):
    return pl.BlockSpec(shape, lambda *_: (0,) * len(shape))


def hbm(shape, dtype=BF16):
    return pltpu.HBM(shape, dtype)


def call(kernel, grid, in_specs, out_specs, out_shape, flops, scratch=(), limit=24):
    return pl.pallas_call(
        kernel,
        grid_spec=pltpu.PrefetchScalarGridSpec(
            num_scalar_prefetch=1,
            grid=grid,
            in_specs=in_specs,
            out_specs=out_specs,
            scratch_shapes=list(scratch),
        ),
        out_shape=out_shape,
        compiler_params=pltpu.CompilerParams(vmem_limit_bytes=limit * MIB),
        cost_estimate=pl.CostEstimate(flops=flops, bytes_accessed=10 * MIB, transcendentals=0),
    )


def place(index, own, behind, top, bottom, before, store):
    rows = own.shape[0]
    half = rows // 2
    store(lax.rem(index, 4), 0, own)
    store(lax.rem(index + 1, 4), 0, behind)
    store(lax.rem(index + 2, 4), 0, top)
    store(lax.rem(index + 2, 4), half, bottom)
    store(lax.rem(index + 3, 4), 0, before)


def place_eight(index, blocks, store):
    groups = blocks[0].shape[0] // 16
    steps = (0, 1, 2, 3, 4, 4, 5, 6, 7)
    for block, step in zip(blocks, steps):
        z = lax.rem(index + step, NZ)
        first = groups // 2 if block is blocks[5] else 0
        for k in range(block.shape[0] // 16):
            start = pl.multiple_of((first + k) * NZ * 16 + z * 16, 16)
            store(start, block[k * 16 : (k + 1) * 16, :])


def gate_up_kernel(index, tok_a, *refs):
    blocks, (gate_a, gate_b, up_a, up_b, out, tok_b) = refs[:9], refs[9:]
    step = pl.program_id(0)

    @pl.when(step == 0)
    def _():
        def store(start, value):
            tok_b[pl.ds(start, 16), :] = value

        place_eight(index[0], blocks, store)

    def part(one, two):
        total = dot(tok_a[...], one[...], NN) + dot(tok_b[...], two[...], NN)
        out[...] = total.astype(BF16)

    @pl.when(step < pl.num_programs(0) // 2)
    def _():
        part(gate_a, gate_b)

    @pl.when(step >= pl.num_programs(0) // 2)
    def _():
        part(up_a, up_b)


def columns(rows, width, at):
    return pl.BlockSpec((rows, width), lambda *_: (0, at))


def gate_up_product(index, own, blocks, gate_a, gate_b, up_a, up_b):
    rows = own.shape[0]
    width, cols = gate_a.shape
    tile = 256
    steps = cols // tile
    first = pl.BlockSpec((width, tile), lambda j, _: (0, jnp.minimum(j, steps - 1)))
    second = pl.BlockSpec((width, tile), lambda j, _: (0, jnp.maximum(j - steps, 0)))
    return call(
        gate_up_kernel,
        (2 * steps,),
        [columns(rows, width, 0)]
        + [columns(block.shape[0], width, 0) for block in blocks]
        + [first, first, second, second],
        [pl.BlockSpec((rows, tile), lambda j, _: (0, j)), whole((rows, width))],
        [hbm((rows, 2 * cols)), hbm((rows, width))],
        8 * rows * width * cols,
    )(index, own, *blocks, gate_a, gate_b, up_a, up_b)


def hidden_term_kernel(index, grad_a, *refs):
    blocks, (down_a, down_b, out, grad_b) = refs[:9], refs[9:]

    @pl.when(pl.program_id(0) == 0)
    def _():
        def store(start, value):
            grad_b[pl.ds(start, 16), :] = value

        place_eight(index[0], blocks, store)

    total = dot(grad_a[...], down_a[...], NT) + dot(grad_b[...], down_b[...], NT)
    out[...] = total.astype(BF16)


def hidden_term_product(index, own, blocks, down_a, down_b):
    rows = own.shape[0]
    cols, width = down_a.shape
    tile = 256
    weight = pl.BlockSpec((tile, width), lambda j, _: (j, 0))
    return call(
        hidden_term_kernel,
        (cols // tile,),
        [columns(rows, width, 1)]
        + [columns(block.shape[0], width, 1) for block in blocks]
        + [weight, weight],
        [pl.BlockSpec((rows, tile), lambda j, _: (0, j)), whole((rows, width))],
        [hbm((rows, cols)), hbm((rows, width))],
        4 * rows * width * cols,
    )(index, own, *blocks, down_a, down_b)


def mixed_kernel(index, own, behind, top, bottom, before, down_a, down_b, out, hidden):
    step = pl.program_id(0)
    rows = own.shape[0]

    @pl.when(step == 0)
    def _():
        def store(block, first, value):
            start = pl.multiple_of(block * rows + first, rows // 2)
            hidden[pl.ds(start, value.shape[0]), :] = value[...]

        place(index[0], own, behind, top, bottom, before, store)

    @pl.when(step < pl.num_programs(0) // 2)
    def _():
        out[...] = dot(hidden[...], down_a[...], NN).astype(BF16)

    @pl.when(step >= pl.num_programs(0) // 2)
    def _():
        out[...] = dot(hidden[...], down_b[...], NN).astype(BF16)


def mixed_product(index, blocks, down_a, down_b):
    rows, depth = blocks[0].shape
    width = down_a.shape[1]
    tile = 512
    steps = width // tile
    shape = (4 * rows, depth)
    return call(
        mixed_kernel,
        (2 * steps,),
        [whole(block.shape) for block in blocks]
        + [
            pl.BlockSpec((depth, tile), lambda j, _: (0, jnp.minimum(j, steps - 1))),
            pl.BlockSpec((depth, tile), lambda j, _: (0, jnp.maximum(j - steps, 0))),
        ],
        [pl.BlockSpec((4 * rows, tile), lambda j, _: (0, j)), whole(shape)],
        [hbm((4 * rows, 2 * width)), hbm(shape)],
        16 * rows * depth * width,
    )(index, *blocks, down_a, down_b)


def input_kernel(
    index, own, behind, top, bottom, before, gate_a, up_a, gate_b, up_b, out, pre_gate, pre_up
):
    step = pl.program_id(0)
    rows = own.shape[0]
    cols = own.shape[1] // 2

    @pl.when(step == 0)
    def _():
        def store(block, first, value):
            start = pl.multiple_of(block * rows + first, rows // 2)
            pre_gate[pl.ds(start, value.shape[0]), :] = value[:, :cols]
            pre_up[pl.ds(start, value.shape[0]), :] = value[:, cols:]

        place(index[0], own, behind, top, bottom, before, store)

    def part(gate, up):
        total = dot(pre_gate[...], gate[...], NT) + dot(pre_up[...], up[...], NT)
        out[...] = total.astype(BF16)

    @pl.when(step < pl.num_programs(0) // 2)
    def _():
        part(gate_a, up_a)

    @pl.when(step >= pl.num_programs(0) // 2)
    def _():
        part(gate_b, up_b)


def input_product(index, blocks, gate_a, up_a, gate_b, up_b):
    rows = blocks[0].shape[0]
    width, cols = gate_a.shape
    tile = 256
    steps = width // tile
    first = pl.BlockSpec((tile, cols), lambda j, _: (jnp.minimum(j, steps - 1), 0))
    second = pl.BlockSpec((tile, cols), lambda j, _: (jnp.maximum(j - steps, 0), 0))
    half = hbm((4 * rows, cols))
    return call(
        input_kernel,
        (2 * steps,),
        [whole(block.shape) for block in blocks] + [first, first, second, second],
        [pl.BlockSpec((4 * rows, tile), lambda j, _: (0, j))] + [whole((4 * rows, cols))] * 2,
        [hbm((4 * rows, 2 * width)), half, half],
        32 * rows * cols * width,
    )(index, *blocks, gate_a, up_a, gate_b, up_b)


def total_of(terms):
    total = terms[0].astype(F32)
    for k in range(1, terms.shape[0]):
        total = total + terms[k].astype(F32)
    return total


def hidden_kernel(index, terms, gate_up, hidden):
    del index
    total = total_of(terms)
    cols = hidden.shape[1]
    gate, up = total[:, :cols], total[:, cols:]
    gate_up[...] = total
    hidden[...] = (gate * jax.nn.sigmoid(gate) * up).astype(BF16)


def hidden_of(index, terms):
    _, rows, cols = terms.shape
    return call(
        hidden_kernel,
        (1,),
        [whole(terms.shape)],
        [whole((rows, cols)), whole((rows, cols // 2))],
        [
            jax.ShapeDtypeStruct((rows, cols), F32),
            jax.ShapeDtypeStruct((rows, cols // 2), BF16),
        ],
        16 * rows * cols,
    )(index, terms)


def pre_kernel(index, terms, gate_up, out):
    del index
    hidden_grad = total_of(terms)
    cols = hidden_grad.shape[1]
    gate, up = gate_up[:, :cols], gate_up[:, cols:]
    sig = jax.nn.sigmoid(gate)
    out[:, :cols] = (hidden_grad * up * sig * (1.0 + gate * (1.0 - sig))).astype(BF16)
    out[:, cols:] = (hidden_grad * gate * sig).astype(BF16)


def pre_grads(index, terms, gate_up):
    return call(
        pre_kernel,
        (1,),
        [whole(terms.shape), whole(gate_up.shape)],
        whole(gate_up.shape),
        jax.ShapeDtypeStruct(gate_up.shape, BF16),
        16 * gate_up.size,
    )(index, terms, gate_up)


def sums_kernel(index, one, two, out):
    del index
    cols = one.shape[2]
    out[:, :cols] = total_of(one).astype(BF16)
    out[:, cols:] = total_of(two).astype(BF16)


def sums_of(index, one, two):
    _, rows, cols = one.shape
    return call(
        sums_kernel,
        (1,),
        [whole(one.shape), whole(two.shape)],
        whole((rows, 2 * cols)),
        jax.ShapeDtypeStruct((rows, 2 * cols), BF16),
        16 * rows * cols,
    )(index, one, two)


def body(tokens, gate_weight, up_weight, down_weight, out_grad):
    core = lax.axis_index("row") % NC
    x = (lax.axis_index("row") // NC).astype(jnp.int32).reshape(1)
    z = (lax.axis_index("col") // NY).astype(jnp.int32).reshape(1)
    half = tokens.shape[0] // NC
    width = tokens.shape[1]

    def halves(value):
        mine = lax.dynamic_slice_in_dim(value, core * half, half, 0)
        other = lax.dynamic_slice_in_dim(value, (1 - core) * half, half, 0)
        return mine, swap_core(other)

    def join(value):
        mine = value[:, :width]
        got = swap_core(value[:, width:])
        first = jnp.where(core == 0, mine, got)
        second = jnp.where(core == 0, got, mine)
        return jnp.concatenate([first, second], axis=0)

    tok_a, tok_b = halves(tokens)
    grad_a, grad_b = halves(out_grad)
    own = jnp.concatenate([tok_a, grad_a], axis=1)
    other = jnp.concatenate([tok_b, grad_b], axis=1)
    gate_other = swap_core(gate_weight)
    up_other = swap_core(up_weight)
    down_other = swap_core(down_weight)

    other_y = share(other, "col", Y_GROUPS)
    other_blocks = ring_eight(other_y, "col", Z_UP, Z_DOWN)
    own_z = share(after(own, other_y), "col", Z_GROUPS)
    own_all = share(after(own_z, other_blocks[1], other_blocks[8]), "col", Y_GROUPS)

    gate_up_term, tok_other = gate_up_product(
        z, own_all, other_blocks, gate_weight, gate_other, up_weight, up_other
    )
    gate_up, hidden_own = hidden_of(z, exchange(gate_up_term, "row", X_GROUPS))
    hidden_term, grad_other = hidden_term_product(
        z, own_all, other_blocks, down_weight, down_other
    )
    pre_own = pre_grads(x, exchange(hidden_term, "row", X_GROUPS), gate_up)

    hidden_blocks = ring_blocks(hidden_own, "row", X_UP, X_DOWN)
    mixed_term, hidden = mixed_product(after(x, pre_own), hidden_blocks, down_weight, down_other)
    pre_blocks = ring_blocks(after(pre_own, *hidden_blocks), "row", X_UP, X_DOWN)
    input_term, pre_gate, pre_up = input_product(
        after(x, mixed_term), pre_blocks, gate_weight, up_weight, gate_other, up_other
    )
    mixed_y = exchange(mixed_term, "col", Y_GROUPS)
    input_y = exchange(after(input_term, mixed_y), "col", Y_GROUPS)
    def all_tokens(value):
        return jnp.concatenate([value, swap_core(value)], axis=0)

    tok_rows = jnp.concatenate([own_all[:, :width], swap_core(tok_other)], axis=0)
    grad_rows = jnp.concatenate([own_all[:, width:], swap_core(grad_other)], axis=0)
    down_grad = dot(all_tokens(hidden), grad_rows, TN).astype(BF16)
    gate_grad = dot(tok_rows, all_tokens(pre_gate), TN).astype(BF16)
    up_grad = dot(tok_rows, all_tokens(pre_up), TN).astype(BF16)
    sums = sums_of(x, mixed_y, after(input_y, down_grad))
    sums = exchange(sums, "col", Z_GROUPS).astype(F32).sum(0).astype(BF16)
    mixed = join(sums[:, : 2 * width])
    input_grad = join(sums[:, 2 * width :])

    return (mixed, input_grad, gate_grad, up_grad, down_grad)


def solution(mesh):
    in_specs = (P("col", "row"), P("row", "col"), P("row", "col"), P("col", "row"), P("col", "row"))
    out_specs = (
        P("col", "row"),
        P("col", "row"),
        P("row", "col"),
        P("row", "col"),
        P("col", "row"),
    )
    return jax.shard_map(body, mesh=mesh, in_specs=in_specs, out_specs=out_specs, check_vma=False)
```

```python
import jax
import jax.numpy as jnp
from jax import lax
from jax.experimental import pallas as pl
from jax.experimental.pallas import tpu as pltpu
from jax.sharding import PartitionSpec as P

BF16 = jnp.bfloat16
F32 = jnp.float32
NX, NC, NZ, NY = 4, 2, 8, 4
MIB = 1024 * 1024
LIMIT = 24
TILE = 256

X_GROUPS = [[x * NC + c for x in range(NX)] for c in range(NC)]
Y_GROUPS = [[z * NY + y for y in range(NY)] for z in range(NZ)]
Z_GROUPS = [[z * NY + y for z in range(NZ)] for y in range(NY)]
Y_STEP = [
    [(z * NY + y, z * NY + (y + k) % NY) for z in range(NZ) for y in range(NY)] for k in range(NY)
]
Z_UP = [(z * NY + y, (z + 1) % NZ * NY + y) for z in range(NZ) for y in range(NY)]
Z_DOWN = [(dst, src) for src, dst in Z_UP]
X_UP = [(x * NC + c, (x + 1) % NX * NC + c) for x in range(NX) for c in range(NC)]
X_DOWN = [(dst, src) for src, dst in X_UP]
CORE_PAIRS = [(r, r ^ 1) for r in range(NX * NC)]

NN = (((1,), (0,)), ((), ()))
NT = (((1,), (1,)), ((), ()))
TN = (((0,), (0,)), ((), ()))


def dot(left, right, dims):
    return lax.dot_general(left, right, dims, preferred_element_type=F32)


def swap_core(value):
    return lax.ppermute(value, "row", CORE_PAIRS)


def exchange(value, axis, groups):
    count = len(groups[0])
    got = lax.all_to_all(value, axis, 0, 0, axis_index_groups=groups, tiled=True)
    return got.reshape(count, value.shape[0] // count, value.shape[1])


def share(value, axis, groups):
    got = exchange(jnp.tile(value, (len(groups[0]), 1)), axis, groups)
    return got.reshape(-1, value.shape[1])


def after(value, *others):
    return lax.optimization_barrier((value,) + others)[0]


def ring_blocks(own, axis, up, down):
    half = own.shape[0] // 2
    before = lax.ppermute(own, axis, up)
    behind = lax.ppermute(own, axis, down)
    top = lax.ppermute(before[:half], axis, up)
    bottom = lax.ppermute(behind[half:], axis, down)
    return own, behind, top, bottom, before


def ring_eight(own, axis, up, down):
    half = own.shape[0] // 2
    before, behind = [own], [own]
    for _ in range(3):
        before.append(lax.ppermute(before[-1], axis, up))
        behind.append(lax.ppermute(behind[-1], axis, down))
    top = lax.ppermute(before[3][:half], axis, up)
    bottom = lax.ppermute(behind[3][half:], axis, down)
    behind[2:3], before[2:3] = [in_hbm(behind[2])], [in_hbm(before[2])]
    return own, behind[1], behind[2], behind[3], top, bottom, before[3], before[2], before[1]


def whole(shape):
    return pl.BlockSpec(shape, lambda *_: (0,) * len(shape))


def hbm(shape, dtype=BF16):
    return pltpu.HBM(shape, dtype)


def in_hbm(value):
    return pltpu.with_memory_space_constraint(value, pltpu.HBM)


def call(kernel, grid, in_specs, out_specs, out_shape, flops, scratch=(), limit=LIMIT):
    return pl.pallas_call(
        kernel,
        grid_spec=pltpu.PrefetchScalarGridSpec(
            num_scalar_prefetch=1,
            grid=grid,
            in_specs=in_specs,
            out_specs=out_specs,
            scratch_shapes=list(scratch),
        ),
        out_shape=out_shape,
        compiler_params=pltpu.CompilerParams(vmem_limit_bytes=limit * MIB),
        cost_estimate=pl.CostEstimate(flops=flops, bytes_accessed=10 * MIB, transcendentals=0),
    )


def place(index, own, behind, top, bottom, before, store):
    rows = own.shape[0]
    half = rows // 2
    store(lax.rem(index, 4), 0, own)
    store(lax.rem(index + 1, 4), 0, behind)
    store(lax.rem(index + 2, 4), 0, top)
    store(lax.rem(index + 2, 4), half, bottom)
    store(lax.rem(index + 3, 4), 0, before)


def place_eight(index, blocks, store):
    steps = (0, 1, 2, 3, 4, 4, 5, 6, 7)
    for block, step in zip(blocks, steps):
        z = lax.rem(index[0] + step, NZ)
        first = NY // 2 if block is blocks[5] else 0
        for k in range(block.shape[0] // 16):
            y = lax.rem(index[1] + first + k, NY)
            start = pl.multiple_of(y * NZ * 16 + z * 16, 16)
            store(start, block[k * 16 : (k + 1) * 16, :])


def gate_up_kernel(index, tok_a, *refs):
    blocks, (gate_a, gate_b, up_a, up_b, out, tok_b) = refs[:9], refs[9:]
    step = pl.program_id(0)

    @pl.when(step == 0)
    def _():
        def store(start, value):
            tok_b[pl.ds(start, 16), :] = value

        place_eight(index, blocks, store)

    tile = gate_a.shape[1]
    gate = dot(tok_a[...], gate_a[...], NN) + dot(tok_b[...], gate_b[...], NN)
    out[:, :tile] = gate.astype(BF16)
    up = dot(tok_a[...], up_a[...], NN) + dot(tok_b[...], up_b[...], NN)
    out[:, tile:] = up.astype(BF16)


def columns(rows, width, at):
    return pl.BlockSpec((rows, width), lambda *_: (0, at))


def gate_up_product(index, own, blocks, gate_a, gate_b, up_a, up_b):
    rows = own.shape[0]
    width, cols = gate_a.shape
    weight = pl.BlockSpec((width, TILE), lambda j, _: (0, j))
    return call(
        gate_up_kernel,
        (cols // TILE,),
        [columns(rows, width, 0)]
        + [columns(block.shape[0], width, 0) for block in blocks]
        + [weight] * 4,
        [pl.BlockSpec((rows, 2 * TILE), lambda j, _: (0, j)), whole((rows, width))],
        [hbm((rows, 2 * cols)), hbm((rows, width))],
        8 * rows * width * cols,
    )(index, own, *blocks, gate_a, gate_b, up_a, up_b)


def hidden_term_kernel(index, grad_a, *refs):
    blocks, (down_a, down_b, out, grad_b) = refs[:9], refs[9:]

    @pl.when(pl.program_id(0) == 0)
    def _():
        def store(start, value):
            grad_b[pl.ds(start, 16), :] = value

        place_eight(index, blocks, store)

    total = dot(grad_a[...], down_a[...], NT) + dot(grad_b[...], down_b[...], NT)
    out[...] = total.astype(BF16)


def hidden_term_product(index, own, blocks, down_a, down_b):
    rows = own.shape[0]
    cols, width = down_a.shape
    tile = 384
    weight = pl.BlockSpec((tile, width), lambda j, _: (j, 0))
    return call(
        hidden_term_kernel,
        (cols // tile,),
        [columns(rows, width, 1)]
        + [columns(block.shape[0], width, 1) for block in blocks]
        + [weight, weight],
        [pl.BlockSpec((rows, tile), lambda j, _: (0, j)), whole((rows, width))],
        [hbm((rows, cols)), hbm((rows, width))],
        4 * rows * width * cols,
    )(index, own, *blocks, down_a, down_b)


def mixed_kernel(index, own, behind, top, bottom, before, down_a, down_b, out, hidden):
    step = pl.program_id(0)
    rows = own.shape[0]

    @pl.when(step == 0)
    def _():
        def store(block, first, value):
            start = pl.multiple_of(block * rows + first, rows // 2)
            hidden[pl.ds(start, value.shape[0]), :] = value[...]

        place(index[0], own, behind, top, bottom, before, store)

    @pl.when(step < pl.num_programs(0) // 2)
    def _():
        out[...] = dot(hidden[...], down_a[...], NN).astype(BF16)

    @pl.when(step >= pl.num_programs(0) // 2)
    def _():
        out[...] = dot(hidden[...], down_b[...], NN).astype(BF16)


def mixed_product(index, blocks, down_a, down_b):
    rows, depth = blocks[0].shape
    width = down_a.shape[1]
    tile = 512
    steps = width // tile
    shape = (4 * rows, depth)
    return call(
        mixed_kernel,
        (2 * steps,),
        [whole(block.shape) for block in blocks]
        + [
            pl.BlockSpec((depth, tile), lambda j, _: (0, jnp.minimum(j, steps - 1))),
            pl.BlockSpec((depth, tile), lambda j, _: (0, jnp.maximum(j - steps, 0))),
        ],
        [pl.BlockSpec((4 * rows, tile), lambda j, _: (0, j)), whole(shape)],
        [hbm((4 * rows, 2 * width)), hbm(shape)],
        16 * rows * depth * width,
    )(index, *blocks, down_a, down_b)


def input_kernel(
    index, own, behind, top, bottom, before, gate_a, up_a, gate_b, up_b, out, pre_gate, pre_up
):
    step = pl.program_id(0)
    rows = own.shape[0]
    cols = own.shape[1] // 2

    @pl.when(step == 0)
    def _():
        def store(block, first, value):
            start = pl.multiple_of(block * rows + first, rows // 2)
            pre_gate[pl.ds(start, value.shape[0]), :] = value[:, :cols]
            pre_up[pl.ds(start, value.shape[0]), :] = value[:, cols:]

        place(index[0], own, behind, top, bottom, before, store)

    def part(gate, up):
        total = dot(pre_gate[...], gate[...], NT) + dot(pre_up[...], up[...], NT)
        out[...] = total.astype(BF16)

    @pl.when(step < pl.num_programs(0) // 2)
    def _():
        part(gate_a, up_a)

    @pl.when(step >= pl.num_programs(0) // 2)
    def _():
        part(gate_b, up_b)


def input_product(index, blocks, gate_a, up_a, gate_b, up_b):
    rows = blocks[0].shape[0]
    width, cols = gate_a.shape
    tile = 512
    steps = width // tile
    first = pl.BlockSpec((tile, cols), lambda j, _: (jnp.minimum(j, steps - 1), 0))
    second = pl.BlockSpec((tile, cols), lambda j, _: (jnp.maximum(j - steps, 0), 0))
    half = hbm((4 * rows, cols))
    return call(
        input_kernel,
        (2 * steps,),
        [whole(block.shape) for block in blocks] + [first, first, second, second],
        [pl.BlockSpec((4 * rows, tile), lambda j, _: (0, j))] + [whole((4 * rows, cols))] * 2,
        [hbm((4 * rows, 2 * width)), half, half],
        32 * rows * cols * width,
    )(index, *blocks, gate_a, up_a, gate_b, up_b)


def total_of(terms):
    total = terms[0].astype(F32)
    for k in range(1, terms.shape[0]):
        total = total + terms[k].astype(F32)
    return total


def hidden_kernel(index, terms, gate_up, hidden):
    del index
    total = total_of(terms)
    gate_up[...] = total
    for k in range(hidden.shape[1] // TILE):
        gate = total[:, 2 * k * TILE : (2 * k + 1) * TILE]
        up = total[:, (2 * k + 1) * TILE : (2 * k + 2) * TILE]
        hidden[:, k * TILE : (k + 1) * TILE] = (gate * jax.nn.sigmoid(gate) * up).astype(BF16)


def hidden_of(index, terms):
    _, rows, cols = terms.shape
    return call(
        hidden_kernel,
        (1,),
        [whole(terms.shape)],
        [whole((rows, cols)), whole((rows, cols // 2))],
        [
            hbm((rows, cols), F32),
            jax.ShapeDtypeStruct((rows, cols // 2), BF16),
        ],
        16 * rows * cols,
    )(index, terms)


def pre_kernel(index, terms, gate_up, out):
    del index
    total = total_of(terms)
    cols = total.shape[1]
    for k in range(cols // TILE):
        hidden_grad = total[:, k * TILE : (k + 1) * TILE]
        gate = gate_up[:, 2 * k * TILE : (2 * k + 1) * TILE]
        up = gate_up[:, (2 * k + 1) * TILE : (2 * k + 2) * TILE]
        sig = jax.nn.sigmoid(gate)
        pre_gate = hidden_grad * up * sig * (1.0 + gate * (1.0 - sig))
        out[:, k * TILE : (k + 1) * TILE] = pre_gate.astype(BF16)
        out[:, cols + k * TILE : cols + (k + 1) * TILE] = (hidden_grad * gate * sig).astype(BF16)


def pre_grads(index, terms, gate_up):
    return call(
        pre_kernel,
        (1,),
        [whole(terms.shape), whole(gate_up.shape)],
        whole(gate_up.shape),
        jax.ShapeDtypeStruct(gate_up.shape, BF16),
        16 * gate_up.size,
    )(index, terms, gate_up)


def sums_kernel(index, one, two, out):
    del index
    cols = one.shape[2]
    out[:, :cols] = total_of(one).astype(BF16)
    out[:, cols:] = total_of(two).astype(BF16)


def sums_of(index, one, two):
    _, rows, cols = one.shape
    return call(
        sums_kernel,
        (1,),
        [whole(one.shape), whole(two.shape)],
        whole((rows, 2 * cols)),
        jax.ShapeDtypeStruct((rows, 2 * cols), BF16),
        16 * rows * cols,
    )(index, one, two)


def body(tokens, gate_weight, up_weight, down_weight, out_grad):
    core = lax.axis_index("row") % NC
    x = (lax.axis_index("row") // NC).astype(jnp.int32).reshape(1)
    col = lax.axis_index("col")
    zy = jnp.stack([col // NY, col % NY]).astype(jnp.int32)
    half = tokens.shape[0] // NC
    width = tokens.shape[1]

    def halves(value):
        mine = lax.dynamic_slice_in_dim(value, core * half, half, 0)
        other = lax.dynamic_slice_in_dim(value, (1 - core) * half, half, 0)
        return mine, swap_core(other)

    def join(value):
        mine = value[:, :width]
        got = swap_core(value[:, width:])
        first = jnp.where(core == 0, mine, got)
        second = jnp.where(core == 0, got, mine)
        return jnp.concatenate([first, second], axis=0)

    tok_a, tok_b = halves(tokens)
    grad_a, grad_b = halves(out_grad)
    own = jnp.concatenate([tok_a, grad_a], axis=1)
    other = jnp.concatenate([tok_b, grad_b], axis=1)
    gate_own, gate_other = in_hbm(gate_weight), in_hbm(swap_core(gate_weight))
    up_own, up_other = in_hbm(up_weight), in_hbm(swap_core(up_weight))
    down_own, down_other = in_hbm(down_weight), in_hbm(swap_core(down_weight))

    other_y = [other] + [lax.ppermute(other, "col", Y_STEP[NY - k]) for k in range(1, NY)]
    other_y = jnp.concatenate(other_y, axis=0)
    other_blocks = ring_eight(other_y, "col", Z_UP, Z_DOWN)
    own_z = share(own, "col", Z_GROUPS)
    own_all = share(after(own_z, other_blocks[1], other_blocks[8]), "col", Y_GROUPS)

    gate_up_term, tok_other = gate_up_product(
        zy, own_all, other_blocks, gate_own, gate_other, up_own, up_other
    )
    gate_up, hidden_own = hidden_of(x, exchange(gate_up_term, "row", X_GROUPS))
    hidden_term, grad_other = hidden_term_product(
        zy, own_all, other_blocks, down_own, down_other
    )
    pre_own = pre_grads(x, exchange(hidden_term, "row", X_GROUPS), gate_up)

    hidden_blocks = ring_blocks(hidden_own, "row", X_UP, X_DOWN)
    mixed_term, hidden = mixed_product(after(x, pre_own), hidden_blocks, down_own, down_other)
    pre_blocks = ring_blocks(after(pre_own, *hidden_blocks), "row", X_UP, X_DOWN)
    input_term, pre_gate, pre_up = input_product(
        after(x, mixed_term), pre_blocks, gate_own, up_own, gate_other, up_other
    )
    mixed_y = exchange(mixed_term, "col", Y_GROUPS)
    input_y = exchange(after(input_term, mixed_y), "col", Y_GROUPS)
    def all_tokens(value):
        return jnp.concatenate([value, swap_core(value)], axis=0)

    tok_rows = jnp.concatenate([own_all[:, :width], swap_core(tok_other)], axis=0)
    grad_rows = jnp.concatenate([own_all[:, width:], swap_core(grad_other)], axis=0)
    down_grad = dot(all_tokens(hidden), grad_rows, TN).astype(BF16)
    gate_grad = dot(tok_rows, all_tokens(pre_gate), TN).astype(BF16)
    up_grad = dot(tok_rows, all_tokens(pre_up), TN).astype(BF16)
    sums = sums_of(x, mixed_y, after(input_y, down_grad, gate_grad))
    sums = after(exchange(sums, "col", Z_GROUPS), up_grad).astype(F32).sum(0).astype(BF16)
    mixed = join(sums[:, : 2 * width])
    input_grad = join(sums[:, 2 * width :])

    return (mixed, input_grad, gate_grad, up_grad, down_grad)


def solution(mesh):
    in_specs = (P("col", "row"), P("row", "col"), P("row", "col"), P("col", "row"), P("col", "row"))
    out_specs = (
        P("col", "row"),
        P("col", "row"),
        P("row", "col"),
        P("row", "col"),
        P("col", "row"),
    )
    return jax.shard_map(body, mesh=mesh, in_specs=in_specs, out_specs=out_specs, check_vma=False)
```

```python
import jax
import jax.numpy as jnp
from jax import lax
from jax.experimental import pallas as pl
from jax.experimental.pallas import tpu as pltpu
from jax.sharding import PartitionSpec as P

BF16 = jnp.bfloat16
F32 = jnp.float32
NX, NC, NZ, NY = 4, 2, 8, 4
MIB = 1024 * 1024
LIMIT = 24
TILE = 256

X_GROUPS = [[x * NC + c for x in range(NX)] for c in range(NC)]
Y_GROUPS = [[z * NY + y for y in range(NY)] for z in range(NZ)]
Z_GROUPS = [[z * NY + y for z in range(NZ)] for y in range(NY)]
Y_STEP = [
    [(z * NY + y, z * NY + (y + k) % NY) for z in range(NZ) for y in range(NY)] for k in range(NY)
]
Z_STEP = [
    [(z * NY + y, (z + k) % NZ * NY + y) for z in range(NZ) for y in range(NY)] for k in range(NZ)
]
Z_UP = [(z * NY + y, (z + 1) % NZ * NY + y) for z in range(NZ) for y in range(NY)]
Z_DOWN = [(dst, src) for src, dst in Z_UP]
X_UP = [(x * NC + c, (x + 1) % NX * NC + c) for x in range(NX) for c in range(NC)]
X_DOWN = [(dst, src) for src, dst in X_UP]
CORE_PAIRS = [(r, r ^ 1) for r in range(NX * NC)]

NN = (((1,), (0,)), ((), ()))
NT = (((1,), (1,)), ((), ()))
TN = (((0,), (0,)), ((), ()))


def dot(left, right, dims):
    return lax.dot_general(left, right, dims, preferred_element_type=F32)


def swap_core(value):
    return lax.ppermute(value, "row", CORE_PAIRS)


def exchange(value, axis, groups):
    count = len(groups[0])
    got = lax.all_to_all(value, axis, 0, 0, axis_index_groups=groups, tiled=True)
    return got.reshape(count, value.shape[0] // count, value.shape[1])


def share(value, axis, groups):
    got = exchange(jnp.tile(value, (len(groups[0]), 1)), axis, groups)
    return got.reshape(-1, value.shape[1])


def after(value, *others):
    return lax.optimization_barrier((value,) + others)[0]


def ring_blocks(own, axis, up, down):
    half = own.shape[0] // 2
    before = lax.ppermute(own, axis, up)
    behind = lax.ppermute(own, axis, down)
    top = lax.ppermute(before[:half], axis, up)
    bottom = lax.ppermute(behind[half:], axis, down)
    return own, behind, top, bottom, before


def ring_eight(own, axis, up, down):
    half = own.shape[0] // 2
    before, behind = [own], [own]
    for _ in range(3):
        before.append(lax.ppermute(before[-1], axis, up))
        behind.append(lax.ppermute(behind[-1], axis, down))
    top = lax.ppermute(before[3][:half], axis, up)
    bottom = lax.ppermute(behind[3][half:], axis, down)
    behind[2:3], before[2:3] = [in_hbm(behind[2])], [in_hbm(before[2])]
    return own, behind[1], behind[2], behind[3], top, bottom, before[3], before[2], before[1]


def whole(shape):
    return pl.BlockSpec(shape, lambda *_: (0,) * len(shape))


def hbm(shape, dtype=BF16):
    return pltpu.HBM(shape, dtype)


def in_hbm(value):
    return pltpu.with_memory_space_constraint(value, pltpu.HBM)


def call(kernel, grid, in_specs, out_specs, out_shape, flops, scratch=(), limit=LIMIT):
    return pl.pallas_call(
        kernel,
        grid_spec=pltpu.PrefetchScalarGridSpec(
            num_scalar_prefetch=1,
            grid=grid,
            in_specs=in_specs,
            out_specs=out_specs,
            scratch_shapes=list(scratch),
        ),
        out_shape=out_shape,
        compiler_params=pltpu.CompilerParams(vmem_limit_bytes=limit * MIB),
        cost_estimate=pl.CostEstimate(flops=flops, bytes_accessed=10 * MIB, transcendentals=0),
    )


def place(index, own, behind, top, bottom, before, store):
    rows = own.shape[0]
    half = rows // 2
    store(lax.rem(index, 4), 0, own)
    store(lax.rem(index + 1, 4), 0, behind)
    store(lax.rem(index + 2, 4), 0, top)
    store(lax.rem(index + 2, 4), half, bottom)
    store(lax.rem(index + 3, 4), 0, before)


def place_eight(index, blocks, store):
    steps = (0, 1, 2, 3, 4, 4, 5, 6, 7)
    for block, step in zip(blocks, steps):
        z = lax.rem(index[0] + step, NZ)
        first = NY // 2 if block is blocks[5] else 0
        for k in range(block.shape[0] // 16):
            y = lax.rem(index[1] + first + k, NY)
            start = pl.multiple_of(y * NZ * 16 + z * 16, 16)
            store(start, block[k * 16 : (k + 1) * 16, :])


def gate_up_kernel(index, tok_a, *refs):
    blocks, (gate_a, gate_b, up_a, up_b, out, tok_b) = refs[:9], refs[9:]
    step = pl.program_id(0)

    @pl.when(step == 0)
    def _():
        def store(start, value):
            tok_b[pl.ds(start, 16), :] = value

        place_eight(index, blocks, store)

    tile = gate_a.shape[1]
    gate = dot(tok_a[...], gate_a[...], NN) + dot(tok_b[...], gate_b[...], NN)
    out[:, :tile] = gate.astype(BF16)
    up = dot(tok_a[...], up_a[...], NN) + dot(tok_b[...], up_b[...], NN)
    out[:, tile:] = up.astype(BF16)


def columns(rows, width, at):
    return pl.BlockSpec((rows, width), lambda *_: (0, at))


def gate_up_product(index, own, blocks, gate_a, gate_b, up_a, up_b):
    rows = own.shape[0]
    width, cols = gate_a.shape
    weight = pl.BlockSpec((width, TILE), lambda j, _: (0, j))
    return call(
        gate_up_kernel,
        (cols // TILE,),
        [columns(rows, width, 0)]
        + [columns(block.shape[0], width, 0) for block in blocks]
        + [weight] * 4,
        [pl.BlockSpec((rows, 2 * TILE), lambda j, _: (0, j)), whole((rows, width))],
        [hbm((rows, 2 * cols)), hbm((rows, width))],
        8 * rows * width * cols,
    )(index, own, *blocks, gate_a, gate_b, up_a, up_b)


def hidden_term_kernel(index, grad_a, *refs):
    blocks, (down_a, down_b, out, grad_b) = refs[:9], refs[9:]

    @pl.when(pl.program_id(0) == 0)
    def _():
        def store(start, value):
            grad_b[pl.ds(start, 16), :] = value

        place_eight(index, blocks, store)

    total = dot(grad_a[...], down_a[...], NT) + dot(grad_b[...], down_b[...], NT)
    out[...] = total.astype(BF16)


def hidden_term_product(index, own, blocks, down_a, down_b):
    rows = own.shape[0]
    cols, width = down_a.shape
    tile = 384
    weight = pl.BlockSpec((tile, width), lambda j, _: (j, 0))
    return call(
        hidden_term_kernel,
        (cols // tile,),
        [columns(rows, width, 1)]
        + [columns(block.shape[0], width, 1) for block in blocks]
        + [weight, weight],
        [pl.BlockSpec((rows, tile), lambda j, _: (0, j)), whole((rows, width))],
        [hbm((rows, cols)), hbm((rows, width))],
        4 * rows * width * cols,
    )(index, own, *blocks, down_a, down_b)


def mixed_kernel(index, own, behind, top, bottom, before, down_a, down_b, out, hidden):
    step = pl.program_id(0)
    rows = own.shape[0]

    @pl.when(step == 0)
    def _():
        def store(block, first, value):
            start = pl.multiple_of(block * rows + first, rows // 2)
            hidden[pl.ds(start, value.shape[0]), :] = value[...]

        place(index[0], own, behind, top, bottom, before, store)

    tile = down_a.shape[1]
    out[:, :tile] = dot(hidden[...], down_a[...], NN).astype(BF16)
    out[:, tile:] = dot(hidden[...], down_b[...], NN).astype(BF16)


def mixed_product(index, blocks, down_a, down_b):
    rows, depth = blocks[0].shape
    width = down_a.shape[1]
    shape = (4 * rows, depth)
    return call(
        mixed_kernel,
        (width // TILE,),
        [whole(block.shape) for block in blocks]
        + [pl.BlockSpec((depth, TILE), lambda j, _: (0, j))] * 2,
        [pl.BlockSpec((4 * rows, 2 * TILE), lambda j, _: (0, j)), whole(shape)],
        [hbm((4 * rows, 2 * width)), hbm(shape)],
        16 * rows * depth * width,
    )(index, *blocks, down_a, down_b)


def input_kernel(
    index, own, behind, top, bottom, before, gate_a, up_a, gate_b, up_b, out, pre_gate, pre_up
):
    step = pl.program_id(0)
    rows = own.shape[0]
    cols = own.shape[1] // 2

    @pl.when(step == 0)
    def _():
        def store(block, first, value):
            start = pl.multiple_of(block * rows + first, rows // 2)
            pre_gate[pl.ds(start, value.shape[0]), :] = value[:, :cols]
            pre_up[pl.ds(start, value.shape[0]), :] = value[:, cols:]

        place(index[0], own, behind, top, bottom, before, store)

    tile = gate_a.shape[0]
    mine = dot(pre_gate[...], gate_a[...], NT) + dot(pre_up[...], up_a[...], NT)
    out[:, :tile] = mine.astype(BF16)
    other = dot(pre_gate[...], gate_b[...], NT) + dot(pre_up[...], up_b[...], NT)
    out[:, tile:] = other.astype(BF16)


def input_product(index, blocks, gate_a, up_a, gate_b, up_b):
    rows = blocks[0].shape[0]
    width, cols = gate_a.shape
    weight = pl.BlockSpec((TILE, cols), lambda j, _: (j, 0))
    half = hbm((4 * rows, cols))
    return call(
        input_kernel,
        (width // TILE,),
        [whole(block.shape) for block in blocks] + [weight] * 4,
        [pl.BlockSpec((4 * rows, 2 * TILE), lambda j, _: (0, j))] + [whole((4 * rows, cols))] * 2,
        [hbm((4 * rows, 2 * width)), half, half],
        32 * rows * cols * width,
    )(index, *blocks, gate_a, up_a, gate_b, up_b)


def total_of(terms):
    total = terms[0].astype(F32)
    for k in range(1, terms.shape[0]):
        total = total + terms[k].astype(F32)
    return total


def hidden_kernel(index, terms, gate_up, hidden):
    del index
    total = total_of(terms)
    gate_up[...] = total
    for k in range(hidden.shape[1] // TILE):
        gate = total[:, 2 * k * TILE : (2 * k + 1) * TILE]
        up = total[:, (2 * k + 1) * TILE : (2 * k + 2) * TILE]
        hidden[:, k * TILE : (k + 1) * TILE] = (gate * jax.nn.sigmoid(gate) * up).astype(BF16)


def hidden_of(index, terms):
    _, rows, cols = terms.shape
    return call(
        hidden_kernel,
        (1,),
        [whole(terms.shape)],
        [whole((rows, cols)), whole((rows, cols // 2))],
        [
            hbm((rows, cols), F32),
            jax.ShapeDtypeStruct((rows, cols // 2), BF16),
        ],
        16 * rows * cols,
    )(index, terms)


def pre_kernel(index, terms, gate_up, out):
    del index
    total = total_of(terms)
    cols = total.shape[1]
    for k in range(cols // TILE):
        hidden_grad = total[:, k * TILE : (k + 1) * TILE]
        gate = gate_up[:, 2 * k * TILE : (2 * k + 1) * TILE]
        up = gate_up[:, (2 * k + 1) * TILE : (2 * k + 2) * TILE]
        sig = jax.nn.sigmoid(gate)
        pre_gate = hidden_grad * up * sig * (1.0 + gate * (1.0 - sig))
        out[:, k * TILE : (k + 1) * TILE] = pre_gate.astype(BF16)
        out[:, cols + k * TILE : cols + (k + 1) * TILE] = (hidden_grad * gate * sig).astype(BF16)


def pre_grads(index, terms, gate_up):
    return call(
        pre_kernel,
        (1,),
        [whole(terms.shape), whole(gate_up.shape)],
        whole(gate_up.shape),
        jax.ShapeDtypeStruct(gate_up.shape, BF16),
        16 * gate_up.size,
    )(index, terms, gate_up)


def store_sum(terms, out):
    width = out.shape[1] // 2
    for k in range(width // TILE):
        mine = terms[:, :, 2 * k * TILE : (2 * k + 1) * TILE]
        other = terms[:, :, (2 * k + 1) * TILE : (2 * k + 2) * TILE]
        out[:, k * TILE : (k + 1) * TILE] = total_of(mine).astype(BF16)
        out[:, width + k * TILE : width + (k + 1) * TILE] = total_of(other).astype(BF16)


def sum_kernel(index, terms, out):
    del index
    store_sum(terms, out)


def sum_of(index, terms):
    _, rows, cols = terms.shape
    return call(
        sum_kernel,
        (1,),
        [whole(terms.shape)],
        whole((rows, cols)),
        hbm((rows, cols)),
        8 * rows * cols,
    )(index, terms)


def split_kernel(index, terms, *refs):
    blocks, total = refs[:NZ], refs[NZ]
    store_sum(terms, total)
    rows = blocks[0].shape[0]
    for k, block in enumerate(blocks):
        start = pl.multiple_of(lax.rem(index[0] + k, NZ) * rows, 16)
        block[...] = total[pl.ds(start, rows), :]


def split_sum(index, terms):
    _, rows, cols = terms.shape
    block = (rows // NZ, cols)
    return call(
        split_kernel,
        (1,),
        [whole(terms.shape)],
        [whole(block)] * NZ,
        [jax.ShapeDtypeStruct(block, BF16)] * NZ,
        8 * rows * cols,
        [pltpu.VMEM((rows, cols), BF16)],
    )(index, terms)


def body(tokens, gate_weight, up_weight, down_weight, out_grad):
    core = lax.axis_index("row") % NC
    x = (lax.axis_index("row") // NC).astype(jnp.int32).reshape(1)
    col = lax.axis_index("col")
    zy = jnp.stack([col // NY, col % NY]).astype(jnp.int32)
    half = tokens.shape[0] // NC
    width = tokens.shape[1]

    def halves(value):
        mine = lax.dynamic_slice_in_dim(value, core * half, half, 0)
        other = lax.dynamic_slice_in_dim(value, (1 - core) * half, half, 0)
        return mine, swap_core(other)

    def join(value):
        mine = value[:, :width]
        got = swap_core(value[:, width:])
        first = jnp.where(core == 0, mine, got)
        second = jnp.where(core == 0, got, mine)
        return jnp.concatenate([first, second], axis=0)

    tok_a, tok_b = halves(tokens)
    grad_a, grad_b = halves(out_grad)
    own = jnp.concatenate([tok_a, grad_a], axis=1)
    other = jnp.concatenate([tok_b, grad_b], axis=1)
    gate_own, gate_other = in_hbm(gate_weight), in_hbm(swap_core(gate_weight))
    up_own, up_other = in_hbm(up_weight), in_hbm(swap_core(up_weight))
    down_own, down_other = in_hbm(down_weight), in_hbm(swap_core(down_weight))

    other_y = [other] + [lax.ppermute(other, "col", Y_STEP[NY - k]) for k in range(1, NY)]
    other_y = jnp.concatenate(other_y, axis=0)
    other_blocks = ring_eight(other_y, "col", Z_UP, Z_DOWN)
    own_z = share(own, "col", Z_GROUPS)
    own_all = share(after(own_z, other_blocks[1], other_blocks[8]), "col", Y_GROUPS)

    gate_up_term, tok_other = gate_up_product(
        zy, own_all, other_blocks, gate_own, gate_other, up_own, up_other
    )
    gate_up, hidden_own = hidden_of(x, exchange(gate_up_term, "row", X_GROUPS))
    hidden_term, grad_other = hidden_term_product(
        zy, own_all, other_blocks, down_own, down_other
    )
    pre_own = pre_grads(x, exchange(hidden_term, "row", X_GROUPS), in_hbm(gate_up))

    hidden_blocks = ring_blocks(hidden_own, "row", X_UP, X_DOWN)
    hidden_blocks = [in_hbm(block) for block in hidden_blocks[:2]] + list(hidden_blocks[2:])
    mixed_term, hidden = mixed_product(after(x, pre_own), hidden_blocks, down_own, down_other)
    pre_blocks = ring_blocks(after(pre_own, hidden_blocks[1], hidden_blocks[4]), "row", X_UP, X_DOWN)
    input_term, pre_gate, pre_up = input_product(
        after(x, mixed_term), pre_blocks, gate_own, up_own, gate_other, up_other
    )
    mixed_y = exchange(mixed_term, "col", Y_GROUPS)
    input_y = exchange(after(input_term, mixed_y), "col", Y_GROUPS)
    def all_tokens(value):
        return jnp.concatenate([value, swap_core(value)], axis=0)

    tok_rows = jnp.concatenate([own_all[:, :width], swap_core(tok_other)], axis=0)
    grad_rows = jnp.concatenate([own_all[:, width:], swap_core(grad_other)], axis=0)
    down_grad = dot(all_tokens(hidden), grad_rows, TN).astype(BF16)
    gate_grad = dot(tok_rows, all_tokens(pre_gate), TN).astype(BF16)
    up_grad = dot(tok_rows, all_tokens(pre_up), TN).astype(BF16)
    mixed_blocks = split_sum(zy, mixed_y)
    mixed_sum = mixed_blocks[0].astype(F32)
    for k in range(1, NZ):
        mixed_sum += lax.ppermute(mixed_blocks[k], "col", Z_STEP[k]).astype(F32)
    mixed = join(mixed_sum.astype(BF16))
    input_sum = sum_of(x, after(input_y, down_grad, mixed))
    input_sum = after(exchange(input_sum, "col", Z_GROUPS), gate_grad, up_grad)
    input_grad = join(input_sum.astype(F32).sum(0).astype(BF16))
    return (mixed, input_grad, gate_grad, up_grad, down_grad)


def solution(mesh):
    in_specs = (P("col", "row"), P("row", "col"), P("row", "col"), P("col", "row"), P("col", "row"))
    out_specs = (
        P("col", "row"),
        P("col", "row"),
        P("row", "col"),
        P("row", "col"),
        P("col", "row"),
    )
    return jax.shard_map(body, mesh=mesh, in_specs=in_specs, out_specs=out_specs, check_vma=False)
```

```python
import jax
import jax.numpy as jnp
from jax import lax
from jax.experimental import pallas as pl
from jax.experimental.pallas import tpu as pltpu
from jax.sharding import PartitionSpec as P

BF16 = jnp.bfloat16
F32 = jnp.float32
NX, NC, NZ, NY = 4, 2, 8, 4
MIB = 1024 * 1024
LIMIT = 24
TILE = 256

X_GROUPS = [[x * NC + c for x in range(NX)] for c in range(NC)]
Y_GROUPS = [[z * NY + y for y in range(NY)] for z in range(NZ)]
Z_GROUPS = [[z * NY + y for z in range(NZ)] for y in range(NY)]
Y_STEP = [
    [(z * NY + y, z * NY + (y + k) % NY) for z in range(NZ) for y in range(NY)] for k in range(NY)
]
Z_STEP = [
    [(z * NY + y, (z + k) % NZ * NY + y) for z in range(NZ) for y in range(NY)] for k in range(NZ)
]
Z_UP = [(z * NY + y, (z + 1) % NZ * NY + y) for z in range(NZ) for y in range(NY)]
Z_DOWN = [(dst, src) for src, dst in Z_UP]
X_STEP = [
    [(x * NC + c, (x + k) % NX * NC + c) for x in range(NX) for c in range(NC)] for k in range(NX)
]
CORE_PAIRS = [(r, r ^ 1) for r in range(NX * NC)]

NN = (((1,), (0,)), ((), ()))
NT = (((1,), (1,)), ((), ()))
TN = (((0,), (0,)), ((), ()))


def dot(left, right, dims):
    return lax.dot_general(left, right, dims, preferred_element_type=F32)


def swap_core(value):
    return lax.ppermute(value, "row", CORE_PAIRS)


def exchange(value, axis, groups):
    count = len(groups[0])
    got = lax.all_to_all(value, axis, 0, 0, axis_index_groups=groups, tiled=True)
    return got.reshape(count, value.shape[0] // count, value.shape[1])


def share(value, axis, groups):
    got = exchange(jnp.tile(value, (len(groups[0]), 1)), axis, groups)
    return got.reshape(-1, value.shape[1])


def after(value, *others):
    return lax.optimization_barrier((value,) + others)[0]


def gather_blocks(own, axis, steps):
    count = len(steps)
    return [own] + [lax.ppermute(own, axis, steps[count - k]) for k in range(1, count)]


def ring_eight(own, axis, up, down):
    half = own.shape[0] // 2
    before, behind = [own], [own]
    for _ in range(3):
        before.append(lax.ppermute(before[-1], axis, up))
        behind.append(lax.ppermute(behind[-1], axis, down))
    top = lax.ppermute(before[3][:half], axis, up)
    bottom = lax.ppermute(behind[3][half:], axis, down)
    behind[2:3], before[2:3] = [in_hbm(behind[2])], [in_hbm(before[2])]
    return own, behind[1], behind[2], behind[3], top, bottom, before[3], before[2], before[1]


def whole(shape):
    return pl.BlockSpec(shape, lambda *_: (0,) * len(shape))


def hbm(shape, dtype=BF16):
    return pltpu.HBM(shape, dtype)


def in_hbm(value):
    return pltpu.with_memory_space_constraint(value, pltpu.HBM)


def call(kernel, grid, in_specs, out_specs, out_shape, flops, scratch=(), limit=LIMIT):
    return pl.pallas_call(
        kernel,
        grid_spec=pltpu.PrefetchScalarGridSpec(
            num_scalar_prefetch=1,
            grid=grid,
            in_specs=in_specs,
            out_specs=out_specs,
            scratch_shapes=list(scratch),
        ),
        out_shape=out_shape,
        compiler_params=pltpu.CompilerParams(vmem_limit_bytes=limit * MIB),
        cost_estimate=pl.CostEstimate(flops=flops, bytes_accessed=10 * MIB, transcendentals=0),
    )


def place(index, blocks, store):
    rows = blocks[0].shape[0]
    for k, block in enumerate(blocks):
        start = pl.multiple_of(lax.rem(index + k, len(blocks)) * rows, rows)
        store(start, block)


def place_eight(index, blocks, store):
    steps = (0, 1, 2, 3, 4, 4, 5, 6, 7)
    for block, step in zip(blocks, steps):
        z = lax.rem(index[0] + step, NZ)
        first = NY // 2 if block is blocks[5] else 0
        for k in range(block.shape[0] // 16):
            y = lax.rem(index[1] + first + k, NY)
            start = pl.multiple_of(y * NZ * 16 + z * 16, 16)
            store(start, block[k * 16 : (k + 1) * 16, :])


def gate_up_kernel(index, tok_a, *refs):
    blocks, (gate_a, gate_b, up_a, up_b, out, tok_b) = refs[:9], refs[9:]
    step = pl.program_id(0)

    @pl.when(step == 0)
    def _():
        def store(start, value):
            tok_b[pl.ds(start, 16), :] = value

        place_eight(index, blocks, store)

    tile = gate_a.shape[1]
    gate = dot(tok_a[...], gate_a[...], NN) + dot(tok_b[...], gate_b[...], NN)
    out[:, :tile] = gate.astype(BF16)
    up = dot(tok_a[...], up_a[...], NN) + dot(tok_b[...], up_b[...], NN)
    out[:, tile:] = up.astype(BF16)


def columns(rows, width, at):
    return pl.BlockSpec((rows, width), lambda *_: (0, at))


def gate_up_product(index, own, blocks, gate_a, gate_b, up_a, up_b):
    rows = own.shape[0]
    width, cols = gate_a.shape
    weight = pl.BlockSpec((width, TILE), lambda j, _: (0, j))
    return call(
        gate_up_kernel,
        (cols // TILE,),
        [columns(rows, width, 0)]
        + [columns(block.shape[0], width, 0) for block in blocks]
        + [weight] * 4,
        [pl.BlockSpec((rows, 2 * TILE), lambda j, _: (0, j)), whole((rows, width))],
        [hbm((rows, 2 * cols)), hbm((rows, width))],
        8 * rows * width * cols,
    )(index, own, *blocks, gate_a, gate_b, up_a, up_b)


def hidden_term_kernel(index, grad_a, *refs):
    blocks, (down_a, down_b, out, grad_b) = refs[:9], refs[9:]

    @pl.when(pl.program_id(0) == 0)
    def _():
        def store(start, value):
            grad_b[pl.ds(start, 16), :] = value

        place_eight(index, blocks, store)

    total = dot(grad_a[...], down_a[...], NT) + dot(grad_b[...], down_b[...], NT)
    out[...] = total.astype(BF16)


def hidden_term_product(index, own, blocks, down_a, down_b):
    rows = own.shape[0]
    cols, width = down_a.shape
    tile = 384
    weight = pl.BlockSpec((tile, width), lambda j, _: (j, 0))
    return call(
        hidden_term_kernel,
        (cols // tile,),
        [columns(rows, width, 1)]
        + [columns(block.shape[0], width, 1) for block in blocks]
        + [weight, weight],
        [pl.BlockSpec((rows, tile), lambda j, _: (0, j)), whole((rows, width))],
        [hbm((rows, cols)), hbm((rows, width))],
        4 * rows * width * cols,
    )(index, own, *blocks, down_a, down_b)


def mixed_kernel(index, *refs):
    blocks, (down_a, down_b, out, hidden) = refs[:NX], refs[NX:]
    step = pl.program_id(0)

    @pl.when(step == 0)
    def _():
        def store(start, value):
            hidden[pl.ds(start, value.shape[0]), :] = value[...]

        place(index[0], blocks, store)

    tile = down_a.shape[1]
    out[:, :tile] = dot(hidden[...], down_a[...], NN).astype(BF16)
    out[:, tile:] = dot(hidden[...], down_b[...], NN).astype(BF16)


def mixed_product(index, blocks, down_a, down_b):
    rows, depth = blocks[0].shape
    width = down_a.shape[1]
    shape = (4 * rows, depth)
    return call(
        mixed_kernel,
        (width // TILE,),
        [whole(block.shape) for block in blocks]
        + [pl.BlockSpec((depth, TILE), lambda j, _: (0, j))] * 2,
        [pl.BlockSpec((4 * rows, 2 * TILE), lambda j, _: (0, j)), whole(shape)],
        [hbm((4 * rows, 2 * width)), hbm(shape)],
        16 * rows * depth * width,
    )(index, *blocks, down_a, down_b)


def input_kernel(index, *refs):
    blocks, (gate_a, up_a, gate_b, up_b, out, pre_gate, pre_up) = refs[:NX], refs[NX:]
    step = pl.program_id(0)
    cols = blocks[0].shape[1] // 2

    @pl.when(step == 0)
    def _():
        def store(start, value):
            pre_gate[pl.ds(start, value.shape[0]), :] = value[:, :cols]
            pre_up[pl.ds(start, value.shape[0]), :] = value[:, cols:]

        place(index[0], blocks, store)

    tile = gate_a.shape[0]
    mine = dot(pre_gate[...], gate_a[...], NT) + dot(pre_up[...], up_a[...], NT)
    out[:, :tile] = mine.astype(BF16)
    other = dot(pre_gate[...], gate_b[...], NT) + dot(pre_up[...], up_b[...], NT)
    out[:, tile:] = other.astype(BF16)


def input_product(index, blocks, gate_a, up_a, gate_b, up_b):
    rows = blocks[0].shape[0]
    width, cols = gate_a.shape
    weight = pl.BlockSpec((TILE, cols), lambda j, _: (j, 0))
    half = hbm((4 * rows, cols))
    return call(
        input_kernel,
        (width // TILE,),
        [whole(block.shape) for block in blocks] + [weight] * 4,
        [pl.BlockSpec((4 * rows, 2 * TILE), lambda j, _: (0, j))] + [whole((4 * rows, cols))] * 2,
        [hbm((4 * rows, 2 * width)), half, half],
        32 * rows * cols * width,
    )(index, *blocks, gate_a, up_a, gate_b, up_b)


def total_of(terms):
    total = terms[0].astype(F32)
    for k in range(1, terms.shape[0]):
        total = total + terms[k].astype(F32)
    return total


def hidden_kernel(index, terms, gate_up, hidden):
    del index
    total = total_of(terms)
    gate_up[...] = total
    for k in range(hidden.shape[1] // TILE):
        gate = total[:, 2 * k * TILE : (2 * k + 1) * TILE]
        up = total[:, (2 * k + 1) * TILE : (2 * k + 2) * TILE]
        hidden[:, k * TILE : (k + 1) * TILE] = (gate * jax.nn.sigmoid(gate) * up).astype(BF16)


def hidden_of(index, terms):
    _, rows, cols = terms.shape
    return call(
        hidden_kernel,
        (1,),
        [whole(terms.shape)],
        [whole((rows, cols)), whole((rows, cols // 2))],
        [
            hbm((rows, cols), F32),
            jax.ShapeDtypeStruct((rows, cols // 2), BF16),
        ],
        16 * rows * cols,
    )(index, terms)


def pre_kernel(index, terms, gate_up, out):
    del index
    total = total_of(terms)
    cols = total.shape[1]
    for k in range(cols // TILE):
        hidden_grad = total[:, k * TILE : (k + 1) * TILE]
        gate = gate_up[:, 2 * k * TILE : (2 * k + 1) * TILE]
        up = gate_up[:, (2 * k + 1) * TILE : (2 * k + 2) * TILE]
        sig = jax.nn.sigmoid(gate)
        pre_gate = hidden_grad * up * sig * (1.0 + gate * (1.0 - sig))
        out[:, k * TILE : (k + 1) * TILE] = pre_gate.astype(BF16)
        out[:, cols + k * TILE : cols + (k + 1) * TILE] = (hidden_grad * gate * sig).astype(BF16)


def pre_grads(index, terms, gate_up):
    return call(
        pre_kernel,
        (1,),
        [whole(terms.shape), whole(gate_up.shape)],
        whole(gate_up.shape),
        jax.ShapeDtypeStruct(gate_up.shape, BF16),
        16 * gate_up.size,
    )(index, terms, gate_up)


def store_sum(terms, out):
    width = out.shape[1] // 2
    for k in range(width // TILE):
        mine = terms[:, :, 2 * k * TILE : (2 * k + 1) * TILE]
        other = terms[:, :, (2 * k + 1) * TILE : (2 * k + 2) * TILE]
        out[:, k * TILE : (k + 1) * TILE] = total_of(mine).astype(BF16)
        out[:, width + k * TILE : width + (k + 1) * TILE] = total_of(other).astype(BF16)


def sum_kernel(index, terms, out):
    del index
    store_sum(terms, out)


def sum_of(index, terms):
    _, rows, cols = terms.shape
    return call(
        sum_kernel,
        (1,),
        [whole(terms.shape)],
        whole((rows, cols)),
        hbm((rows, cols)),
        8 * rows * cols,
    )(index, terms)


def split_kernel(index, terms, near, far, total):
    store_sum(terms, total)
    rows = near.shape[0] // 4
    for k in range(4):
        for step, out in ((k + NZ - 1, near), (k + 3, far)):
            start = pl.multiple_of(lax.rem(index[0] + step, NZ) * rows, 16)
            out[k * rows : (k + 1) * rows, :] = total[pl.ds(start, rows), :]


def split_sum(index, terms):
    _, rows, cols = terms.shape
    half = (rows // 2, cols)
    return call(
        split_kernel,
        (1,),
        [whole(terms.shape)],
        [whole(half)] * 2,
        [jax.ShapeDtypeStruct(half, BF16)] * 2,
        8 * rows * cols,
        [pltpu.VMEM((rows, cols), BF16)],
    )(index, terms)


def fold_kernel(index, near, far, *outs):
    del index
    total = (near[...].astype(F32) + far[...].astype(F32)).astype(BF16)
    rows = outs[0].shape[0]
    for k, out in enumerate(outs):
        out[...] = total[k * rows : (k + 1) * rows, :]


def fold(index, near, far):
    rows, cols = near.shape
    block = (rows // 4, cols)
    return call(
        fold_kernel,
        (1,),
        [whole(near.shape)] * 2,
        [whole(block)] * 4,
        [jax.ShapeDtypeStruct(block, BF16)] * 4,
        8 * rows * cols,
    )(index, near, far)


def body(tokens, gate_weight, up_weight, down_weight, out_grad):
    core = lax.axis_index("row") % NC
    x = (lax.axis_index("row") // NC).astype(jnp.int32).reshape(1)
    col = lax.axis_index("col")
    zy = jnp.stack([col // NY, col % NY]).astype(jnp.int32)
    half = tokens.shape[0] // NC
    width = tokens.shape[1]

    def halves(value):
        mine = lax.dynamic_slice_in_dim(value, core * half, half, 0)
        other = lax.dynamic_slice_in_dim(value, (1 - core) * half, half, 0)
        return mine, swap_core(other)

    def join(value):
        mine = value[:, :width]
        got = swap_core(value[:, width:])
        first = jnp.where(core == 0, mine, got)
        second = jnp.where(core == 0, got, mine)
        return jnp.concatenate([first, second], axis=0)

    tok_a, tok_b = halves(tokens)
    grad_a, grad_b = halves(out_grad)
    own = jnp.concatenate([tok_a, grad_a], axis=1)
    other = jnp.concatenate([tok_b, grad_b], axis=1)
    gate_own, gate_other = in_hbm(gate_weight), in_hbm(swap_core(gate_weight))
    up_own, up_other = in_hbm(up_weight), in_hbm(swap_core(up_weight))
    down_own, down_other = in_hbm(down_weight), in_hbm(swap_core(down_weight))

    other_y = jnp.concatenate(gather_blocks(other, "col", Y_STEP), axis=0)
    other_blocks = ring_eight(other_y, "col", Z_UP, Z_DOWN)
    own_z = share(own, "col", Z_GROUPS)
    own_all = share(after(own_z, other_blocks[1], other_blocks[8]), "col", Y_GROUPS)

    gate_up_term, tok_other = gate_up_product(
        zy, own_all, other_blocks, gate_own, gate_other, up_own, up_other
    )
    gate_up, hidden_own = hidden_of(x, exchange(gate_up_term, "row", X_GROUPS))
    hidden_term, grad_other = hidden_term_product(
        zy, own_all, other_blocks, down_own, down_other
    )
    pre_own = pre_grads(x, exchange(hidden_term, "row", X_GROUPS), in_hbm(gate_up))

    hidden_blocks = gather_blocks(hidden_own, "row", X_STEP)
    mixed_term, hidden = mixed_product(after(x, pre_own), hidden_blocks, down_own, down_other)
    pre_blocks = gather_blocks(after(pre_own, *hidden_blocks[1:]), "row", X_STEP)
    input_term, pre_gate, pre_up = input_product(
        after(x, mixed_term), pre_blocks, gate_own, up_own, gate_other, up_other
    )
    mixed_y = exchange(mixed_term, "col", Y_GROUPS)
    input_y = exchange(after(input_term, mixed_y), "col", Y_GROUPS)
    def all_tokens(value):
        return jnp.concatenate([value, swap_core(value)], axis=0)

    tok_rows = jnp.concatenate([own_all[:, :width], swap_core(tok_other)], axis=0)
    grad_rows = jnp.concatenate([own_all[:, width:], swap_core(grad_other)], axis=0)
    down_grad = dot(all_tokens(hidden), grad_rows, TN).astype(BF16)
    gate_grad = dot(tok_rows, all_tokens(pre_gate), TN).astype(BF16)
    up_grad = dot(tok_rows, all_tokens(pre_up), TN).astype(BF16)
    near, far = split_sum(zy, mixed_y)
    previous, mine, following, second = fold(zy, near, lax.ppermute(far, "col", Z_STEP[4]))
    mixed_sum = mine.astype(F32)
    for block, step in ((previous, NZ - 1), (following, 1), (second, 2)):
        mixed_sum += lax.ppermute(block, "col", Z_STEP[step]).astype(F32)
    mixed = join(mixed_sum.astype(BF16))
    input_sum = sum_of(x, after(input_y, mixed))
    input_sum = after(exchange(input_sum, "col", Z_GROUPS), down_grad, gate_grad, up_grad)
    input_grad = join(input_sum.astype(F32).sum(0).astype(BF16))
    return (mixed, input_grad, gate_grad, up_grad, down_grad)


def solution(mesh):
    in_specs = (P("col", "row"), P("row", "col"), P("row", "col"), P("col", "row"), P("col", "row"))
    out_specs = (
        P("col", "row"),
        P("col", "row"),
        P("row", "col"),
        P("row", "col"),
        P("col", "row"),
    )
    return jax.shard_map(body, mesh=mesh, in_specs=in_specs, out_specs=out_specs, check_vma=False)
```

```python
import jax
import jax.numpy as jnp
from jax import lax
from jax.experimental import pallas as pl
from jax.experimental.pallas import tpu as pltpu
from jax.sharding import PartitionSpec as P

BF16 = jnp.bfloat16
F32 = jnp.float32
NX, NC, NZ, NY = 4, 2, 8, 4
MIB = 1024 * 1024
LIMIT = 24
TILE = 256

X_GROUPS = [[x * NC + c for x in range(NX)] for c in range(NC)]
Y_GROUPS = [[z * NY + y for y in range(NY)] for z in range(NZ)]
Z_GROUPS = [[z * NY + y for z in range(NZ)] for y in range(NY)]
Y_STEP = [
    [(z * NY + y, z * NY + (y + k) % NY) for z in range(NZ) for y in range(NY)] for k in range(NY)
]
Z_STEP = [
    [(z * NY + y, (z + k) % NZ * NY + y) for z in range(NZ) for y in range(NY)] for k in range(NZ)
]
Z_UP = [(z * NY + y, (z + 1) % NZ * NY + y) for z in range(NZ) for y in range(NY)]
Z_DOWN = [(dst, src) for src, dst in Z_UP]
X_STEP = [
    [(x * NC + c, (x + k) % NX * NC + c) for x in range(NX) for c in range(NC)] for k in range(NX)
]
CORE_PAIRS = [(r, r ^ 1) for r in range(NX * NC)]

NN = (((1,), (0,)), ((), ()))
NT = (((1,), (1,)), ((), ()))
TN = (((0,), (0,)), ((), ()))


def dot(left, right, dims):
    return lax.dot_general(left, right, dims, preferred_element_type=F32)


def swap_core(value):
    return lax.ppermute(value, "row", CORE_PAIRS)


def exchange(value, axis, groups):
    count = len(groups[0])
    got = lax.all_to_all(value, axis, 0, 0, axis_index_groups=groups, tiled=True)
    return got.reshape(count, value.shape[0] // count, value.shape[1])


def share(value, axis, groups):
    got = exchange(jnp.tile(value, (len(groups[0]), 1)), axis, groups)
    return got.reshape(-1, value.shape[1])


def after(value, *others):
    return lax.optimization_barrier((value,) + others)[0]


def gather_blocks(own, axis, steps):
    count = len(steps)
    return [own] + [lax.ppermute(own, axis, steps[count - k]) for k in range(1, count)]


def ring_eight(own, axis, up, down):
    half = own.shape[0] // 2
    before, behind = [own], [own]
    for _ in range(3):
        before.append(lax.ppermute(before[-1], axis, up))
        behind.append(lax.ppermute(behind[-1], axis, down))
    top = lax.ppermute(before[3][:half], axis, up)
    bottom = lax.ppermute(behind[3][half:], axis, down)
    behind[2:3], before[2:3] = [in_hbm(behind[2])], [in_hbm(before[2])]
    return own, behind[1], behind[2], behind[3], top, bottom, before[3], before[2], before[1]


def whole(shape):
    return pl.BlockSpec(shape, lambda *_: (0,) * len(shape))


def hbm(shape, dtype=BF16):
    return pltpu.HBM(shape, dtype)


def in_hbm(value):
    return pltpu.with_memory_space_constraint(value, pltpu.HBM)


def call(kernel, grid, in_specs, out_specs, out_shape, flops, scratch=(), limit=LIMIT):
    return pl.pallas_call(
        kernel,
        grid_spec=pltpu.PrefetchScalarGridSpec(
            num_scalar_prefetch=1,
            grid=grid,
            in_specs=in_specs,
            out_specs=out_specs,
            scratch_shapes=list(scratch),
        ),
        out_shape=out_shape,
        compiler_params=pltpu.CompilerParams(vmem_limit_bytes=limit * MIB),
        cost_estimate=pl.CostEstimate(flops=flops, bytes_accessed=10 * MIB, transcendentals=0),
    )


def place(index, blocks, store):
    rows = blocks[0].shape[0]
    for k, block in enumerate(blocks):
        start = pl.multiple_of(lax.rem(index + k, len(blocks)) * rows, rows)
        store(start, block)


def place_eight(index, blocks, store):
    steps = (0, 1, 2, 3, 4, 4, 5, 6, 7)
    for block, step in zip(blocks, steps):
        z = lax.rem(index[0] + step, NZ)
        first = NY // 2 if block is blocks[5] else 0
        for k in range(block.shape[0] // 16):
            y = lax.rem(index[1] + first + k, NY)
            start = pl.multiple_of(y * NZ * 16 + z * 16, 16)
            store(start, block[k * 16 : (k + 1) * 16, :])


def gate_up_kernel(index, tok_a, *refs):
    blocks, (gate_a, gate_b, up_a, up_b, out, tok_b) = refs[:9], refs[9:]
    step = pl.program_id(0)

    @pl.when(step == 0)
    def _():
        def store(start, value):
            tok_b[pl.ds(start, 16), :] = value

        place_eight(index, blocks, store)

    tile = gate_a.shape[1]
    gate = dot(tok_a[...], gate_a[...], NN) + dot(tok_b[...], gate_b[...], NN)
    out[:, :tile] = gate.astype(BF16)
    up = dot(tok_a[...], up_a[...], NN) + dot(tok_b[...], up_b[...], NN)
    out[:, tile:] = up.astype(BF16)


def columns(rows, width, at):
    return pl.BlockSpec((rows, width), lambda *_: (0, at))


def gate_up_product(index, own, blocks, gate_a, gate_b, up_a, up_b):
    rows = own.shape[0]
    width, cols = gate_a.shape
    weight = pl.BlockSpec((width, TILE), lambda j, _: (0, j))
    return call(
        gate_up_kernel,
        (cols // TILE,),
        [columns(rows, width, 0)]
        + [columns(block.shape[0], width, 0) for block in blocks]
        + [weight] * 4,
        [pl.BlockSpec((rows, 2 * TILE), lambda j, _: (0, j)), whole((rows, width))],
        [hbm((rows, 2 * cols)), hbm((rows, width))],
        8 * rows * width * cols,
    )(index, own, *blocks, gate_a, gate_b, up_a, up_b)


def hidden_term_kernel(index, grad_a, *refs):
    blocks, (down_a, down_b) = refs[:9], refs[9:11]
    outs, (grad_b, total) = refs[11 : 11 + NX], refs[11 + NX :]

    @pl.when(pl.program_id(0) == 0)
    def _():
        def store(start, value):
            grad_b[pl.ds(start, 16), :] = value

        place_eight(index, blocks, store)

    term = dot(grad_a[...], down_a[...], NT) + dot(grad_b[...], down_b[...], NT)
    total[...] = term.astype(BF16)
    rows = outs[0].shape[0]
    for k, out in enumerate(outs):
        start = pl.multiple_of(lax.rem(index[2] + k, NX) * rows, rows)
        out[...] = total[pl.ds(start, rows), :]


def hidden_term_product(index, own, blocks, down_a, down_b):
    rows = own.shape[0]
    cols, width = down_a.shape
    tile = 384
    weight = pl.BlockSpec((tile, width), lambda j, _: (j, 0))
    return call(
        hidden_term_kernel,
        (cols // tile,),
        [columns(rows, width, 1)]
        + [columns(block.shape[0], width, 1) for block in blocks]
        + [weight, weight],
        [pl.BlockSpec((rows // NX, tile), lambda j, _: (0, j))] * NX + [whole((rows, width))],
        [hbm((rows // NX, cols))] * NX + [hbm((rows, width))],
        4 * rows * width * cols,
        [pltpu.VMEM((rows, tile), BF16)],
    )(index, own, *blocks, down_a, down_b)


def mixed_kernel(index, *refs):
    blocks, (down_a, down_b, out, hidden) = refs[:NX], refs[NX:]
    step = pl.program_id(0)

    @pl.when(step == 0)
    def _():
        def store(start, value):
            hidden[pl.ds(start, value.shape[0]), :] = value[...]

        place(index[0], blocks, store)

    tile = down_a.shape[1]
    out[:, :tile] = dot(hidden[...], down_a[...], NN).astype(BF16)
    out[:, tile:] = dot(hidden[...], down_b[...], NN).astype(BF16)


def mixed_product(index, blocks, down_a, down_b):
    rows, depth = blocks[0].shape
    width = down_a.shape[1]
    shape = (4 * rows, depth)
    return call(
        mixed_kernel,
        (width // TILE,),
        [whole(block.shape) for block in blocks]
        + [pl.BlockSpec((depth, TILE), lambda j, _: (0, j))] * 2,
        [pl.BlockSpec((4 * rows, 2 * TILE), lambda j, _: (0, j)), whole(shape)],
        [hbm((4 * rows, 2 * width)), hbm(shape)],
        16 * rows * depth * width,
    )(index, *blocks, down_a, down_b)


def input_kernel(index, *refs):
    blocks, (gate_a, up_a, gate_b, up_b, out, pre_gate, pre_up) = refs[:NX], refs[NX:]
    step = pl.program_id(0)
    cols = blocks[0].shape[1] // 2

    @pl.when(step == 0)
    def _():
        def store(start, value):
            pre_gate[pl.ds(start, value.shape[0]), :] = value[:, :cols]
            pre_up[pl.ds(start, value.shape[0]), :] = value[:, cols:]

        place(index[0], blocks, store)

    tile = gate_a.shape[0]
    mine = dot(pre_gate[...], gate_a[...], NT) + dot(pre_up[...], up_a[...], NT)
    out[:, :tile] = mine.astype(BF16)
    other = dot(pre_gate[...], gate_b[...], NT) + dot(pre_up[...], up_b[...], NT)
    out[:, tile:] = other.astype(BF16)


def input_product(index, blocks, gate_a, up_a, gate_b, up_b):
    rows = blocks[0].shape[0]
    width, cols = gate_a.shape
    weight = pl.BlockSpec((TILE, cols), lambda j, _: (j, 0))
    half = hbm((4 * rows, cols))
    return call(
        input_kernel,
        (width // TILE,),
        [whole(block.shape) for block in blocks] + [weight] * 4,
        [pl.BlockSpec((4 * rows, 2 * TILE), lambda j, _: (0, j))] + [whole((4 * rows, cols))] * 2,
        [hbm((4 * rows, 2 * width)), half, half],
        32 * rows * cols * width,
    )(index, *blocks, gate_a, up_a, gate_b, up_b)


def total_of(terms):
    total = terms[0].astype(F32)
    for k in range(1, terms.shape[0]):
        total = total + terms[k].astype(F32)
    return total


def hidden_kernel(index, terms, gate_up, hidden):
    del index
    total = total_of(terms)
    gate_up[...] = total
    for k in range(hidden.shape[1] // TILE):
        gate = total[:, 2 * k * TILE : (2 * k + 1) * TILE]
        up = total[:, (2 * k + 1) * TILE : (2 * k + 2) * TILE]
        hidden[:, k * TILE : (k + 1) * TILE] = (gate * jax.nn.sigmoid(gate) * up).astype(BF16)


def hidden_of(index, terms):
    _, rows, cols = terms.shape
    return call(
        hidden_kernel,
        (1,),
        [whole(terms.shape)],
        [whole((rows, cols)), whole((rows, cols // 2))],
        [
            hbm((rows, cols), F32),
            jax.ShapeDtypeStruct((rows, cols // 2), BF16),
        ],
        16 * rows * cols,
    )(index, terms)


def pre_kernel(index, *refs):
    del index
    terms, (gate_up, out) = refs[:NX], refs[NX:]
    cols = terms[0].shape[1]
    for k in range(cols // TILE):
        hidden_grad = terms[0][:, k * TILE : (k + 1) * TILE].astype(F32)
        for term in terms[1:]:
            hidden_grad = hidden_grad + term[:, k * TILE : (k + 1) * TILE].astype(F32)
        gate = gate_up[:, 2 * k * TILE : (2 * k + 1) * TILE]
        up = gate_up[:, (2 * k + 1) * TILE : (2 * k + 2) * TILE]
        sig = jax.nn.sigmoid(gate)
        pre_gate = hidden_grad * up * sig * (1.0 + gate * (1.0 - sig))
        out[:, k * TILE : (k + 1) * TILE] = pre_gate.astype(BF16)
        out[:, cols + k * TILE : cols + (k + 1) * TILE] = (hidden_grad * gate * sig).astype(BF16)


def pre_grads(index, terms, gate_up):
    return call(
        pre_kernel,
        (1,),
        [whole(term.shape) for term in terms] + [whole(gate_up.shape)],
        whole(gate_up.shape),
        jax.ShapeDtypeStruct(gate_up.shape, BF16),
        16 * gate_up.size,
    )(index, *terms, gate_up)


def store_sum(terms, out):
    width = out.shape[1] // 2
    for k in range(width // TILE):
        mine = terms[:, :, 2 * k * TILE : (2 * k + 1) * TILE]
        other = terms[:, :, (2 * k + 1) * TILE : (2 * k + 2) * TILE]
        out[:, k * TILE : (k + 1) * TILE] = total_of(mine).astype(BF16)
        out[:, width + k * TILE : width + (k + 1) * TILE] = total_of(other).astype(BF16)


def sum_kernel(index, terms, out):
    del index
    store_sum(terms, out)


def sum_of(index, terms):
    _, rows, cols = terms.shape
    return call(
        sum_kernel,
        (1,),
        [whole(terms.shape)],
        whole((rows, cols)),
        hbm((rows, cols)),
        8 * rows * cols,
    )(index, terms)


def split_kernel(index, terms, near, far, total):
    store_sum(terms, total)
    rows = near.shape[0] // 4
    for k in range(4):
        for step, out in ((k + NZ - 1, near), (k + 3, far)):
            start = pl.multiple_of(lax.rem(index[0] + step, NZ) * rows, 16)
            out[k * rows : (k + 1) * rows, :] = total[pl.ds(start, rows), :]


def split_sum(index, terms):
    _, rows, cols = terms.shape
    half = (rows // 2, cols)
    return call(
        split_kernel,
        (1,),
        [whole(terms.shape)],
        [whole(half)] * 2,
        [jax.ShapeDtypeStruct(half, BF16)] * 2,
        8 * rows * cols,
        [pltpu.VMEM((rows, cols), BF16)],
    )(index, terms)


def fold_kernel(index, near, far, *outs):
    del index
    total = (near[...].astype(F32) + far[...].astype(F32)).astype(BF16)
    rows = outs[0].shape[0]
    for k, out in enumerate(outs):
        out[...] = total[k * rows : (k + 1) * rows, :]


def fold(index, near, far):
    rows, cols = near.shape
    block = (rows // 4, cols)
    return call(
        fold_kernel,
        (1,),
        [whole(near.shape)] * 2,
        [whole(block)] * 4,
        [jax.ShapeDtypeStruct(block, BF16)] * 4,
        8 * rows * cols,
    )(index, near, far)


def body(tokens, gate_weight, up_weight, down_weight, out_grad):
    core = lax.axis_index("row") % NC
    x = (lax.axis_index("row") // NC).astype(jnp.int32).reshape(1)
    col = lax.axis_index("col")
    zyx = jnp.stack([col // NY, col % NY, lax.axis_index("row") // NC]).astype(jnp.int32)
    half = tokens.shape[0] // NC
    width = tokens.shape[1]

    def halves(value):
        mine = lax.dynamic_slice_in_dim(value, core * half, half, 0)
        other = lax.dynamic_slice_in_dim(value, (1 - core) * half, half, 0)
        return mine, swap_core(other)

    def join(value):
        mine = value[:, :width]
        got = swap_core(value[:, width:])
        first = jnp.where(core == 0, mine, got)
        second = jnp.where(core == 0, got, mine)
        return jnp.concatenate([first, second], axis=0)

    tok_a, tok_b = halves(tokens)
    grad_a, grad_b = halves(out_grad)
    own = jnp.concatenate([tok_a, grad_a], axis=1)
    other = jnp.concatenate([tok_b, grad_b], axis=1)
    gate_own, gate_other = in_hbm(gate_weight), in_hbm(swap_core(gate_weight))
    up_own, up_other = in_hbm(up_weight), in_hbm(swap_core(up_weight))
    down_own, down_other = in_hbm(down_weight), in_hbm(swap_core(down_weight))

    other_y = jnp.concatenate(gather_blocks(other, "col", Y_STEP), axis=0)
    other_blocks = ring_eight(other_y, "col", Z_UP, Z_DOWN)
    own_z = share(own, "col", Z_GROUPS)
    own_all = share(after(own_z, other_blocks[1], other_blocks[8]), "col", Y_GROUPS)

    gate_up_term, tok_other = gate_up_product(
        zyx, own_all, other_blocks, gate_own, gate_other, up_own, up_other
    )
    gate_up, hidden_own = hidden_of(x, exchange(gate_up_term, "row", X_GROUPS))
    *hidden_terms, grad_other = hidden_term_product(
        zyx, own_all, other_blocks, down_own, down_other
    )
    hidden_terms = [in_hbm(hidden_terms[0])] + [
        lax.ppermute(hidden_terms[k], "row", X_STEP[k]) for k in range(1, NX)
    ]
    pre_own = pre_grads(x, hidden_terms, in_hbm(gate_up))

    hidden_blocks = gather_blocks(hidden_own, "row", X_STEP)
    mixed_term, hidden = mixed_product(after(x, pre_own), hidden_blocks, down_own, down_other)
    pre_blocks = gather_blocks(after(pre_own, *hidden_blocks[1:]), "row", X_STEP)
    input_term, pre_gate, pre_up = input_product(
        after(x, mixed_term), pre_blocks, gate_own, up_own, gate_other, up_other
    )
    mixed_y = exchange(mixed_term, "col", Y_GROUPS)
    input_y = exchange(after(input_term, mixed_y), "col", Y_GROUPS)
    def all_tokens(value):
        return jnp.concatenate([value, swap_core(value)], axis=0)

    tok_rows = jnp.concatenate([own_all[:, :width], swap_core(tok_other)], axis=0)
    grad_rows = jnp.concatenate([own_all[:, width:], swap_core(grad_other)], axis=0)
    down_grad = dot(all_tokens(hidden), grad_rows, TN).astype(BF16)
    gate_grad = dot(tok_rows, all_tokens(pre_gate), TN).astype(BF16)
    up_grad = dot(tok_rows, all_tokens(pre_up), TN).astype(BF16)
    near, far = split_sum(zyx, mixed_y)
    previous, mine, following, second = fold(
        zyx, near, after(lax.ppermute(far, "col", Z_STEP[4]), down_grad)
    )
    mixed_sum = mine.astype(F32)
    for block, step in ((previous, NZ - 1), (following, 1), (second, 2)):
        mixed_sum += lax.ppermute(block, "col", Z_STEP[step]).astype(F32)
    mixed = join(mixed_sum.astype(BF16))
    input_sum = sum_of(x, after(input_y, mixed))
    input_sum = after(exchange(input_sum, "col", Z_GROUPS), down_grad, gate_grad, up_grad)
    input_grad = join(input_sum.astype(F32).sum(0).astype(BF16))
    return (mixed, input_grad, gate_grad, up_grad, down_grad)


def solution(mesh):
    in_specs = (P("col", "row"), P("row", "col"), P("row", "col"), P("col", "row"), P("col", "row"))
    out_specs = (
        P("col", "row"),
        P("col", "row"),
        P("row", "col"),
        P("row", "col"),
        P("col", "row"),
    )
    return jax.shard_map(body, mesh=mesh, in_specs=in_specs, out_specs=out_specs, check_vma=False)
```

```python
import jax
import jax.numpy as jnp
from jax import lax
from jax.experimental import pallas as pl
from jax.experimental.pallas import tpu as pltpu
from jax.sharding import PartitionSpec as P

BF16 = jnp.bfloat16
F32 = jnp.float32
NX, NC, NZ, NY = 4, 2, 8, 4
MIB = 1024 * 1024
LIMIT = 24
TILE = 256

X_GROUPS = [[x * NC + c for x in range(NX)] for c in range(NC)]
Y_GROUPS = [[z * NY + y for y in range(NY)] for z in range(NZ)]
Z_GROUPS = [[z * NY + y for z in range(NZ)] for y in range(NY)]
Y_STEP = [
    [(z * NY + y, z * NY + (y + k) % NY) for z in range(NZ) for y in range(NY)] for k in range(NY)
]
Z_STEP = [
    [(z * NY + y, (z + k) % NZ * NY + y) for z in range(NZ) for y in range(NY)] for k in range(NZ)
]
Z_UP = [(z * NY + y, (z + 1) % NZ * NY + y) for z in range(NZ) for y in range(NY)]
Z_DOWN = [(dst, src) for src, dst in Z_UP]
X_STEP = [
    [(x * NC + c, (x + k) % NX * NC + c) for x in range(NX) for c in range(NC)] for k in range(NX)
]
CORE_PAIRS = [(r, r ^ 1) for r in range(NX * NC)]

NN = (((1,), (0,)), ((), ()))
NT = (((1,), (1,)), ((), ()))
TN = (((0,), (0,)), ((), ()))


def dot(left, right, dims):
    return lax.dot_general(left, right, dims, preferred_element_type=F32)


def swap_core(value):
    return lax.ppermute(value, "row", CORE_PAIRS)


def exchange(value, axis, groups):
    count = len(groups[0])
    got = lax.all_to_all(value, axis, 0, 0, axis_index_groups=groups, tiled=True)
    return got.reshape(count, value.shape[0] // count, value.shape[1])


def share(value, axis, groups):
    got = exchange(jnp.tile(value, (len(groups[0]), 1)), axis, groups)
    return got.reshape(-1, value.shape[1])


def after(value, *others):
    return lax.optimization_barrier((value,) + others)[0]


def gather_blocks(own, axis, steps):
    count = len(steps)
    return [own] + [lax.ppermute(own, axis, steps[count - k]) for k in range(1, count)]


def ring_eight(own, axis, up, down):
    half = own.shape[0] // 2
    before, behind = [own], [own]
    for _ in range(3):
        before.append(lax.ppermute(before[-1], axis, up))
        behind.append(lax.ppermute(behind[-1], axis, down))
    top = lax.ppermute(before[3][:half], axis, up)
    bottom = lax.ppermute(behind[3][half:], axis, down)
    behind[2:3], before[2:3] = [in_hbm(behind[2])], [in_hbm(before[2])]
    return own, behind[1], behind[2], behind[3], top, bottom, before[3], before[2], before[1]


def whole(shape):
    return pl.BlockSpec(shape, lambda *_: (0,) * len(shape))


def hbm(shape, dtype=BF16):
    return pltpu.HBM(shape, dtype)


def in_hbm(value):
    return pltpu.with_memory_space_constraint(value, pltpu.HBM)


def call(kernel, grid, in_specs, out_specs, out_shape, flops, scratch=(), limit=LIMIT):
    return pl.pallas_call(
        kernel,
        grid_spec=pltpu.PrefetchScalarGridSpec(
            num_scalar_prefetch=1,
            grid=grid,
            in_specs=in_specs,
            out_specs=out_specs,
            scratch_shapes=list(scratch),
        ),
        out_shape=out_shape,
        compiler_params=pltpu.CompilerParams(vmem_limit_bytes=limit * MIB),
        cost_estimate=pl.CostEstimate(flops=flops, bytes_accessed=10 * MIB, transcendentals=0),
    )


def place(index, blocks, store):
    rows = blocks[0].shape[0]
    for k, block in enumerate(blocks):
        start = pl.multiple_of(lax.rem(index + k, len(blocks)) * rows, rows)
        store(start, block)


def place_eight(index, blocks, store):
    steps = (0, 1, 2, 3, 4, 4, 5, 6, 7)
    for block, step in zip(blocks, steps):
        z = lax.rem(index[0] + step, NZ)
        first = NY // 2 if block is blocks[5] else 0
        for k in range(block.shape[0] // 16):
            y = lax.rem(index[1] + first + k, NY)
            start = pl.multiple_of(y * NZ * 16 + z * 16, 16)
            store(start, block[k * 16 : (k + 1) * 16, :])


def gate_up_kernel(index, tok_a, *refs):
    blocks, (gate_a, gate_b, up_a, up_b, out, tok_b) = refs[:9], refs[9:]
    step = pl.program_id(0)

    @pl.when(step == 0)
    def _():
        def store(start, value):
            tok_b[pl.ds(start, 16), :] = value

        place_eight(index, blocks, store)

    tile = gate_a.shape[1]
    gate = dot(tok_a[...], gate_a[...], NN) + dot(tok_b[...], gate_b[...], NN)
    out[:, :tile] = gate.astype(BF16)
    up = dot(tok_a[...], up_a[...], NN) + dot(tok_b[...], up_b[...], NN)
    out[:, tile:] = up.astype(BF16)


def columns(rows, width, at):
    return pl.BlockSpec((rows, width), lambda *_: (0, at))


def gate_up_product(index, own, blocks, gate_a, gate_b, up_a, up_b):
    rows = own.shape[0]
    width, cols = gate_a.shape
    weight = pl.BlockSpec((width, TILE), lambda j, _: (0, j))
    return call(
        gate_up_kernel,
        (cols // TILE,),
        [columns(rows, width, 0)]
        + [columns(block.shape[0], width, 0) for block in blocks]
        + [weight] * 4,
        [pl.BlockSpec((rows, 2 * TILE), lambda j, _: (0, j)), whole((rows, width))],
        [hbm((rows, 2 * cols)), hbm((rows, width))],
        8 * rows * width * cols,
    )(index, own, *blocks, gate_a, gate_b, up_a, up_b)


def hidden_term_kernel(index, grad_a, *refs):
    blocks, (down_a, down_b) = refs[:9], refs[9:11]
    outs, (grad_b, total) = refs[11 : 11 + NX], refs[11 + NX :]

    @pl.when(pl.program_id(0) == 0)
    def _():
        def store(start, value):
            grad_b[pl.ds(start, 16), :] = value

        place_eight(index, blocks, store)

    term = dot(grad_a[...], down_a[...], NT) + dot(grad_b[...], down_b[...], NT)
    total[...] = term.astype(BF16)
    rows = outs[0].shape[0]
    for k, out in enumerate(outs):
        start = pl.multiple_of(lax.rem(index[2] + k, NX) * rows, rows)
        out[...] = total[pl.ds(start, rows), :]


def hidden_term_product(index, own, blocks, down_a, down_b):
    rows = own.shape[0]
    cols, width = down_a.shape
    tile = 256
    weight = pl.BlockSpec((tile, width), lambda j, _: (j, 0))
    return call(
        hidden_term_kernel,
        (cols // tile,),
        [columns(rows, width, 1)]
        + [columns(block.shape[0], width, 1) for block in blocks]
        + [weight, weight],
        [pl.BlockSpec((rows // NX, tile), lambda j, _: (0, j))] * NX + [whole((rows, width))],
        [hbm((rows // NX, cols))] * NX + [hbm((rows, width))],
        4 * rows * width * cols,
        [pltpu.VMEM((rows, tile), BF16)],
    )(index, own, *blocks, down_a, down_b)


def mixed_kernel(index, *refs):
    blocks, (down_a, down_b, out, hidden) = refs[:NX], refs[NX:]
    step = pl.program_id(0)

    @pl.when(step == 0)
    def _():
        def store(start, value):
            hidden[pl.ds(start, value.shape[0]), :] = value[...]

        place(index[0], blocks, store)

    tile = down_a.shape[1]
    out[:, :tile] = dot(hidden[...], down_a[...], NN).astype(BF16)
    out[:, tile:] = dot(hidden[...], down_b[...], NN).astype(BF16)


def mixed_product(index, blocks, down_a, down_b):
    rows, depth = blocks[0].shape
    width = down_a.shape[1]
    shape = (4 * rows, depth)
    return call(
        mixed_kernel,
        (width // TILE,),
        [whole(block.shape) for block in blocks]
        + [pl.BlockSpec((depth, TILE), lambda j, _: (0, j))] * 2,
        [pl.BlockSpec((4 * rows, 2 * TILE), lambda j, _: (0, j)), whole(shape)],
        [hbm((4 * rows, 2 * width)), hbm(shape)],
        16 * rows * depth * width,
    )(index, *blocks, down_a, down_b)


def input_kernel(index, *refs):
    blocks, (gate_a, up_a, gate_b, up_b, out, pre_gate, pre_up) = refs[:NX], refs[NX:]
    step = pl.program_id(0)
    cols = blocks[0].shape[1] // 2

    @pl.when(step == 0)
    def _():
        def store(start, value):
            pre_gate[pl.ds(start, value.shape[0]), :] = value[:, :cols]
            pre_up[pl.ds(start, value.shape[0]), :] = value[:, cols:]

        place(index[0], blocks, store)

    tile = gate_a.shape[0]
    mine = dot(pre_gate[...], gate_a[...], NT) + dot(pre_up[...], up_a[...], NT)
    out[:, :tile] = mine.astype(BF16)
    other = dot(pre_gate[...], gate_b[...], NT) + dot(pre_up[...], up_b[...], NT)
    out[:, tile:] = other.astype(BF16)


def input_product(index, blocks, gate_a, up_a, gate_b, up_b):
    rows = blocks[0].shape[0]
    width, cols = gate_a.shape
    weight = pl.BlockSpec((TILE, cols), lambda j, _: (j, 0))
    half = hbm((4 * rows, cols))
    return call(
        input_kernel,
        (width // TILE,),
        [whole(block.shape) for block in blocks] + [weight] * 4,
        [pl.BlockSpec((4 * rows, 2 * TILE), lambda j, _: (0, j))] + [whole((4 * rows, cols))] * 2,
        [hbm((4 * rows, 2 * width)), half, half],
        32 * rows * cols * width,
    )(index, *blocks, gate_a, up_a, gate_b, up_b)


def total_of(terms):
    total = terms[0].astype(F32)
    for k in range(1, terms.shape[0]):
        total = total + terms[k].astype(F32)
    return total


def hidden_kernel(index, terms, gate_up, hidden):
    del index
    total = total_of(terms)
    gate_up[...] = total
    for k in range(hidden.shape[1] // TILE):
        gate = total[:, 2 * k * TILE : (2 * k + 1) * TILE]
        up = total[:, (2 * k + 1) * TILE : (2 * k + 2) * TILE]
        hidden[:, k * TILE : (k + 1) * TILE] = (gate * jax.nn.sigmoid(gate) * up).astype(BF16)


def hidden_of(index, terms):
    _, rows, cols = terms.shape
    return call(
        hidden_kernel,
        (1,),
        [whole(terms.shape)],
        [whole((rows, cols)), whole((rows, cols // 2))],
        [
            hbm((rows, cols), F32),
            jax.ShapeDtypeStruct((rows, cols // 2), BF16),
        ],
        16 * rows * cols,
    )(index, terms)


def pre_kernel(index, *refs):
    del index
    terms, (gate_up, out) = refs[:NX], refs[NX:]
    cols = terms[0].shape[1]
    for k in range(cols // TILE):
        hidden_grad = terms[0][:, k * TILE : (k + 1) * TILE].astype(F32)
        for term in terms[1:]:
            hidden_grad = hidden_grad + term[:, k * TILE : (k + 1) * TILE].astype(F32)
        gate = gate_up[:, 2 * k * TILE : (2 * k + 1) * TILE]
        up = gate_up[:, (2 * k + 1) * TILE : (2 * k + 2) * TILE]
        sig = jax.nn.sigmoid(gate)
        pre_gate = hidden_grad * up * sig * (1.0 + gate * (1.0 - sig))
        out[:, k * TILE : (k + 1) * TILE] = pre_gate.astype(BF16)
        out[:, cols + k * TILE : cols + (k + 1) * TILE] = (hidden_grad * gate * sig).astype(BF16)


def pre_grads(index, terms, gate_up):
    return call(
        pre_kernel,
        (1,),
        [whole(term.shape) for term in terms] + [whole(gate_up.shape)],
        whole(gate_up.shape),
        jax.ShapeDtypeStruct(gate_up.shape, BF16),
        16 * gate_up.size,
    )(index, *terms, gate_up)


def store_sum(terms, out):
    width = out.shape[1] // 2
    for k in range(width // TILE):
        mine = terms[:, :, 2 * k * TILE : (2 * k + 1) * TILE]
        other = terms[:, :, (2 * k + 1) * TILE : (2 * k + 2) * TILE]
        out[:, k * TILE : (k + 1) * TILE] = total_of(mine).astype(BF16)
        out[:, width + k * TILE : width + (k + 1) * TILE] = total_of(other).astype(BF16)


def sum_kernel(index, terms, out):
    del index
    store_sum(terms, out)


def sum_of(index, terms):
    _, rows, cols = terms.shape
    return call(
        sum_kernel,
        (1,),
        [whole(terms.shape)],
        whole((rows, cols)),
        hbm((rows, cols)),
        8 * rows * cols,
    )(index, terms)


def split_kernel(index, terms, near, far, total):
    store_sum(terms, total)
    rows = near.shape[0] // 4
    for k in range(4):
        for step, out in ((k + NZ - 1, near), (k + 3, far)):
            start = pl.multiple_of(lax.rem(index[0] + step, NZ) * rows, 16)
            out[k * rows : (k + 1) * rows, :] = total[pl.ds(start, rows), :]


def split_sum(index, terms):
    _, rows, cols = terms.shape
    half = (rows // 2, cols)
    return call(
        split_kernel,
        (1,),
        [whole(terms.shape)],
        [whole(half)] * 2,
        [jax.ShapeDtypeStruct(half, BF16)] * 2,
        8 * rows * cols,
        [pltpu.VMEM((rows, cols), BF16)],
    )(index, terms)


def fold_kernel(index, near, far, *outs):
    del index
    total = (near[...].astype(F32) + far[...].astype(F32)).astype(BF16)
    rows = outs[0].shape[0]
    for k, out in enumerate(outs):
        out[...] = total[k * rows : (k + 1) * rows, :]


def fold(index, near, far):
    rows, cols = near.shape
    block = (rows // 4, cols)
    return call(
        fold_kernel,
        (1,),
        [whole(near.shape)] * 2,
        [whole(block)] * 4,
        [jax.ShapeDtypeStruct(block, BF16)] * 4,
        8 * rows * cols,
    )(index, near, far)


def body(tokens, gate_weight, up_weight, down_weight, out_grad):
    core = lax.axis_index("row") % NC
    x = (lax.axis_index("row") // NC).astype(jnp.int32).reshape(1)
    col = lax.axis_index("col")
    zyx = jnp.stack([col // NY, col % NY, lax.axis_index("row") // NC]).astype(jnp.int32)
    half = tokens.shape[0] // NC
    width = tokens.shape[1]

    def halves(value):
        mine = lax.dynamic_slice_in_dim(value, core * half, half, 0)
        other = lax.dynamic_slice_in_dim(value, (1 - core) * half, half, 0)
        return mine, swap_core(other)

    def join(value):
        mine = value[:, :width]
        got = swap_core(value[:, width:])
        first = jnp.where(core == 0, mine, got)
        second = jnp.where(core == 0, got, mine)
        return jnp.concatenate([first, second], axis=0)

    tok_a, tok_b = halves(tokens)
    grad_a, grad_b = halves(out_grad)
    own = jnp.concatenate([tok_a, grad_a], axis=1)
    other = jnp.concatenate([tok_b, grad_b], axis=1)
    gate_own, gate_other = in_hbm(gate_weight), in_hbm(swap_core(gate_weight))
    up_own, up_other = in_hbm(up_weight), in_hbm(swap_core(up_weight))
    down_own, down_other = in_hbm(down_weight), in_hbm(swap_core(down_weight))

    other_y = jnp.concatenate(gather_blocks(other, "col", Y_STEP), axis=0)
    other_blocks = ring_eight(other_y, "col", Z_UP, Z_DOWN)
    own_z = share(own, "col", Z_GROUPS)
    own_all = share(after(own_z, other_blocks[1], other_blocks[8]), "col", Y_GROUPS)

    gate_up_term, tok_other = gate_up_product(
        zyx, own_all, other_blocks, gate_own, gate_other, up_own, up_other
    )
    gate_up, hidden_own = hidden_of(x, exchange(gate_up_term, "row", X_GROUPS))
    *hidden_terms, grad_other = hidden_term_product(
        zyx, own_all, other_blocks, down_own, down_other
    )
    hidden_terms = [in_hbm(hidden_terms[0])] + [
        lax.ppermute(hidden_terms[k], "row", X_STEP[k]) for k in range(1, NX)
    ]
    pre_own = pre_grads(x, hidden_terms, in_hbm(gate_up))

    hidden_blocks = gather_blocks(hidden_own, "row", X_STEP)
    mixed_term, hidden = mixed_product(after(x, pre_own), hidden_blocks, down_own, down_other)
    pre_blocks = gather_blocks(after(pre_own, *hidden_blocks[1:]), "row", X_STEP)
    input_term, pre_gate, pre_up = input_product(
        after(x, mixed_term), pre_blocks, gate_own, up_own, gate_other, up_other
    )
    mixed_y = exchange(mixed_term, "col", Y_GROUPS)
    input_y = exchange(after(input_term, mixed_y), "col", Y_GROUPS)
    def all_tokens(value):
        return jnp.concatenate([value, swap_core(value)], axis=0)

    tok_rows = jnp.concatenate([own_all[:, :width], swap_core(tok_other)], axis=0)
    grad_rows = jnp.concatenate([own_all[:, width:], swap_core(grad_other)], axis=0)
    down_grad = dot(all_tokens(hidden), grad_rows, TN).astype(BF16)
    gate_grad = dot(tok_rows, all_tokens(pre_gate), TN).astype(BF16)
    input_sum = sum_of(x, after(input_y, down_grad, gate_grad))
    up_grad = dot(tok_rows, after(all_tokens(pre_up), input_sum), TN).astype(BF16)
    near, far = split_sum(zyx, mixed_y)
    previous, mine, following, second = fold(
        zyx, near, after(lax.ppermute(far, "col", Z_STEP[4]), up_grad)
    )
    mixed_sum = mine.astype(F32)
    for block, step in ((previous, NZ - 1), (following, 1), (second, 2)):
        mixed_sum += lax.ppermute(block, "col", Z_STEP[step]).astype(F32)
    mixed = join(mixed_sum.astype(BF16))
    input_sum = after(exchange(input_sum, "col", Z_GROUPS), up_grad, mixed)
    input_grad = join(input_sum.astype(F32).sum(0).astype(BF16))
    return (mixed, input_grad, gate_grad, up_grad, down_grad)


def solution(mesh):
    in_specs = (P("col", "row"), P("row", "col"), P("row", "col"), P("col", "row"), P("col", "row"))
    out_specs = (
        P("col", "row"),
        P("col", "row"),
        P("row", "col"),
        P("row", "col"),
        P("col", "row"),
    )
    return jax.shard_map(body, mesh=mesh, in_specs=in_specs, out_specs=out_specs, check_vma=False)
```

```python
import jax
import jax.numpy as jnp
from jax import lax
from jax.experimental import pallas as pl
from jax.experimental.pallas import tpu as pltpu
from jax.sharding import PartitionSpec as P

BF16 = jnp.bfloat16
F32 = jnp.float32
NX, NC, NZ, NY = 4, 2, 8, 4
MIB = 1024 * 1024
LIMIT = 24
TILE = 256

X_GROUPS = [[x * NC + c for x in range(NX)] for c in range(NC)]
Y_GROUPS = [[z * NY + y for y in range(NY)] for z in range(NZ)]
Z_GROUPS = [[z * NY + y for z in range(NZ)] for y in range(NY)]
Y_STEP = [
    [(z * NY + y, z * NY + (y + k) % NY) for z in range(NZ) for y in range(NY)] for k in range(NY)
]
Z_STEP = [
    [(z * NY + y, (z + k) % NZ * NY + y) for z in range(NZ) for y in range(NY)] for k in range(NZ)
]
Z_UP = [(z * NY + y, (z + 1) % NZ * NY + y) for z in range(NZ) for y in range(NY)]
Z_DOWN = [(dst, src) for src, dst in Z_UP]
X_STEP = [
    [(x * NC + c, (x + k) % NX * NC + c) for x in range(NX) for c in range(NC)] for k in range(NX)
]
CORE_PAIRS = [(r, r ^ 1) for r in range(NX * NC)]

NN = (((1,), (0,)), ((), ()))
NT = (((1,), (1,)), ((), ()))
TN = (((0,), (0,)), ((), ()))


def dot(left, right, dims):
    return lax.dot_general(left, right, dims, preferred_element_type=F32)


def swap_core(value):
    return lax.ppermute(value, "row", CORE_PAIRS)


def exchange(value, axis, groups):
    count = len(groups[0])
    got = lax.all_to_all(value, axis, 0, 0, axis_index_groups=groups, tiled=True)
    return got.reshape(count, value.shape[0] // count, value.shape[1])


def share(value, axis, groups):
    got = exchange(jnp.tile(value, (len(groups[0]), 1)), axis, groups)
    return got.reshape(-1, value.shape[1])


def after(value, *others):
    return lax.optimization_barrier((value,) + others)[0]


def gather_blocks(own, axis, steps):
    count = len(steps)
    return [own] + [lax.ppermute(own, axis, steps[count - k]) for k in range(1, count)]


def ring_eight(own, axis, up, down):
    half = own.shape[0] // 2
    before, behind = [own], [own]
    for _ in range(3):
        before.append(lax.ppermute(before[-1], axis, up))
        behind.append(lax.ppermute(behind[-1], axis, down))
    top = lax.ppermute(before[3][:half], axis, up)
    bottom = lax.ppermute(behind[3][half:], axis, down)
    behind[2:3], before[2:3] = [in_hbm(behind[2])], [in_hbm(before[2])]
    return own, behind[1], behind[2], behind[3], top, bottom, before[3], before[2], before[1]


def whole(shape):
    return pl.BlockSpec(shape, lambda *_: (0,) * len(shape))


def hbm(shape, dtype=BF16):
    return pltpu.HBM(shape, dtype)


def in_hbm(value):
    return pltpu.with_memory_space_constraint(value, pltpu.HBM)


def call(kernel, grid, in_specs, out_specs, out_shape, flops, scratch=(), limit=LIMIT):
    return pl.pallas_call(
        kernel,
        grid_spec=pltpu.PrefetchScalarGridSpec(
            num_scalar_prefetch=1,
            grid=grid,
            in_specs=in_specs,
            out_specs=out_specs,
            scratch_shapes=list(scratch),
        ),
        out_shape=out_shape,
        compiler_params=pltpu.CompilerParams(vmem_limit_bytes=limit * MIB),
        cost_estimate=pl.CostEstimate(flops=flops, bytes_accessed=10 * MIB, transcendentals=0),
    )


def place(index, blocks, store):
    rows = blocks[0].shape[0]
    for k, block in enumerate(blocks):
        start = pl.multiple_of(lax.rem(index + k, len(blocks)) * rows, rows)
        store(start, block)


def place_eight(index, blocks, store):
    steps = (0, 1, 2, 3, 4, 4, 5, 6, 7)
    for block, step in zip(blocks, steps):
        z = lax.rem(index[0] + step, NZ)
        first = NY // 2 if block is blocks[5] else 0
        for k in range(block.shape[0] // 16):
            y = lax.rem(index[1] + first + k, NY)
            start = pl.multiple_of(y * NZ * 16 + z * 16, 16)
            store(start, block[k * 16 : (k + 1) * 16, :])


def gate_up_kernel(index, tok_a, *refs):
    blocks, (gate_a, gate_b, up_a, up_b, out, tok_b) = refs[:9], refs[9:]
    step = pl.program_id(0)

    @pl.when(step == 0)
    def _():
        def store(start, value):
            tok_b[pl.ds(start, 16), :] = value

        place_eight(index, blocks, store)

    tile = gate_a.shape[1]
    gate = dot(tok_a[...], gate_a[...], NN) + dot(tok_b[...], gate_b[...], NN)
    out[:, :tile] = gate.astype(BF16)
    up = dot(tok_a[...], up_a[...], NN) + dot(tok_b[...], up_b[...], NN)
    out[:, tile:] = up.astype(BF16)


def columns(rows, width, at):
    return pl.BlockSpec((rows, width), lambda *_: (0, at))


def gate_up_product(index, own, blocks, gate_a, gate_b, up_a, up_b):
    rows = own.shape[0]
    width, cols = gate_a.shape
    weight = pl.BlockSpec((width, TILE), lambda j, _: (0, j))
    return call(
        gate_up_kernel,
        (cols // TILE,),
        [columns(rows, width, 0)]
        + [columns(block.shape[0], width, 0) for block in blocks]
        + [weight] * 4,
        [pl.BlockSpec((rows, 2 * TILE), lambda j, _: (0, j)), whole((rows, width))],
        [hbm((rows, 2 * cols)), hbm((rows, width))],
        8 * rows * width * cols,
    )(index, own, *blocks, gate_a, gate_b, up_a, up_b)


def hidden_term_kernel(index, grad_a, *refs):
    blocks, (down_a, down_b) = refs[:9], refs[9:11]
    outs, (grad_b, total) = refs[11 : 11 + NX], refs[11 + NX :]

    @pl.when(pl.program_id(0) == 0)
    def _():
        def store(start, value):
            grad_b[pl.ds(start, 16), :] = value

        place_eight(index, blocks, store)

    term = dot(grad_a[...], down_a[...], NT) + dot(grad_b[...], down_b[...], NT)
    total[...] = term.astype(BF16)
    rows = outs[0].shape[0]
    for k, out in enumerate(outs):
        start = pl.multiple_of(lax.rem(index[2] + k, NX) * rows, rows)
        out[...] = total[pl.ds(start, rows), :]


def hidden_term_product(index, own, blocks, down_a, down_b):
    rows = own.shape[0]
    cols, width = down_a.shape
    tile = 256
    weight = pl.BlockSpec((tile, width), lambda j, _: (j, 0))
    return call(
        hidden_term_kernel,
        (cols // tile,),
        [columns(rows, width, 1)]
        + [columns(block.shape[0], width, 1) for block in blocks]
        + [weight, weight],
        [pl.BlockSpec((rows // NX, tile), lambda j, _: (0, j))] * NX + [whole((rows, width))],
        [hbm((rows // NX, cols))] * NX + [hbm((rows, width))],
        4 * rows * width * cols,
        [pltpu.VMEM((rows, tile), BF16)],
    )(index, own, *blocks, down_a, down_b)


def mixed_kernel(index, *refs):
    blocks, (down_a, down_b, out, hidden) = refs[:NX], refs[NX:]
    step = pl.program_id(0)

    @pl.when(step == 0)
    def _():
        def store(start, value):
            hidden[pl.ds(start, value.shape[0]), :] = value[...]

        place(index[0], blocks, store)

    tile = down_a.shape[1]
    out[:, :tile] = dot(hidden[...], down_a[...], NN).astype(BF16)
    out[:, tile:] = dot(hidden[...], down_b[...], NN).astype(BF16)


def mixed_product(index, blocks, down_a, down_b):
    rows, depth = blocks[0].shape
    width = down_a.shape[1]
    shape = (4 * rows, depth)
    return call(
        mixed_kernel,
        (width // TILE,),
        [whole(block.shape) for block in blocks]
        + [pl.BlockSpec((depth, TILE), lambda j, _: (0, j))] * 2,
        [pl.BlockSpec((4 * rows, 2 * TILE), lambda j, _: (0, j)), whole(shape)],
        [hbm((4 * rows, 2 * width)), hbm(shape)],
        16 * rows * depth * width,
    )(index, *blocks, down_a, down_b)


def input_kernel(index, *refs):
    blocks, (gate_a, up_a, gate_b, up_b, out, pre_gate, pre_up) = refs[:NX], refs[NX:]
    step = pl.program_id(0)
    cols = blocks[0].shape[1] // 2

    @pl.when(step == 0)
    def _():
        def store(start, value):
            pre_gate[pl.ds(start, value.shape[0]), :] = value[:, :cols]
            pre_up[pl.ds(start, value.shape[0]), :] = value[:, cols:]

        place(index[0], blocks, store)

    tile = gate_a.shape[0]
    mine = dot(pre_gate[...], gate_a[...], NT) + dot(pre_up[...], up_a[...], NT)
    out[:, :tile] = mine.astype(BF16)
    other = dot(pre_gate[...], gate_b[...], NT) + dot(pre_up[...], up_b[...], NT)
    out[:, tile:] = other.astype(BF16)


def input_product(index, blocks, gate_a, up_a, gate_b, up_b):
    rows = blocks[0].shape[0]
    width, cols = gate_a.shape
    weight = pl.BlockSpec((TILE, cols), lambda j, _: (j, 0))
    half = hbm((4 * rows, cols))
    return call(
        input_kernel,
        (width // TILE,),
        [whole(block.shape) for block in blocks] + [weight] * 4,
        [pl.BlockSpec((4 * rows, 2 * TILE), lambda j, _: (0, j))] + [whole((4 * rows, cols))] * 2,
        [hbm((4 * rows, 2 * width)), half, half],
        32 * rows * cols * width,
    )(index, *blocks, gate_a, up_a, gate_b, up_b)


def total_of(terms):
    total = terms[0].astype(F32)
    for k in range(1, terms.shape[0]):
        total = total + terms[k].astype(F32)
    return total


def hidden_kernel(index, terms, gate_up, hidden):
    del index
    total = total_of(terms)
    gate_up[...] = total
    for k in range(hidden.shape[1] // TILE):
        gate = total[:, 2 * k * TILE : (2 * k + 1) * TILE]
        up = total[:, (2 * k + 1) * TILE : (2 * k + 2) * TILE]
        hidden[:, k * TILE : (k + 1) * TILE] = (gate * jax.nn.sigmoid(gate) * up).astype(BF16)


def hidden_of(index, terms):
    _, rows, cols = terms.shape
    return call(
        hidden_kernel,
        (1,),
        [whole(terms.shape)],
        [whole((rows, cols)), whole((rows, cols // 2))],
        [
            hbm((rows, cols), F32),
            jax.ShapeDtypeStruct((rows, cols // 2), BF16),
        ],
        16 * rows * cols,
    )(index, terms)


def pre_kernel(index, *refs):
    del index
    terms, (gate_up, out) = refs[:NX], refs[NX:]
    cols = terms[0].shape[1]
    for k in range(cols // TILE):
        hidden_grad = terms[0][:, k * TILE : (k + 1) * TILE].astype(F32)
        for term in terms[1:]:
            hidden_grad = hidden_grad + term[:, k * TILE : (k + 1) * TILE].astype(F32)
        gate = gate_up[:, 2 * k * TILE : (2 * k + 1) * TILE]
        up = gate_up[:, (2 * k + 1) * TILE : (2 * k + 2) * TILE]
        sig = jax.nn.sigmoid(gate)
        pre_gate = hidden_grad * up * sig * (1.0 + gate * (1.0 - sig))
        out[:, k * TILE : (k + 1) * TILE] = pre_gate.astype(BF16)
        out[:, cols + k * TILE : cols + (k + 1) * TILE] = (hidden_grad * gate * sig).astype(BF16)


def pre_grads(index, terms, gate_up):
    return call(
        pre_kernel,
        (1,),
        [whole(term.shape) for term in terms] + [whole(gate_up.shape)],
        whole(gate_up.shape),
        jax.ShapeDtypeStruct(gate_up.shape, BF16),
        16 * gate_up.size,
    )(index, *terms, gate_up)


def store_sum(terms, out):
    width = out.shape[1] // 2
    for k in range(width // TILE):
        mine = terms[:, :, 2 * k * TILE : (2 * k + 1) * TILE]
        other = terms[:, :, (2 * k + 1) * TILE : (2 * k + 2) * TILE]
        out[:, k * TILE : (k + 1) * TILE] = total_of(mine).astype(BF16)
        out[:, width + k * TILE : width + (k + 1) * TILE] = total_of(other).astype(BF16)


def sum_kernel(index, terms, out):
    del index
    store_sum(terms, out)


def sum_of(index, terms):
    _, rows, cols = terms.shape
    return call(
        sum_kernel,
        (1,),
        [whole(terms.shape)],
        whole((rows, cols)),
        hbm((rows, cols)),
        8 * rows * cols,
    )(index, terms)


def split_kernel(index, terms, near, far, total):
    store_sum(terms, total)
    rows = near.shape[0] // 4
    for k in range(4):
        for step, out in ((k + NZ - 1, near), (k + 3, far)):
            start = pl.multiple_of(lax.rem(index[0] + step, NZ) * rows, 16)
            out[k * rows : (k + 1) * rows, :] = total[pl.ds(start, rows), :]


def split_sum(index, terms):
    _, rows, cols = terms.shape
    half = (rows // 2, cols)
    return call(
        split_kernel,
        (1,),
        [whole(terms.shape)],
        [whole(half)] * 2,
        [jax.ShapeDtypeStruct(half, BF16)] * 2,
        8 * rows * cols,
        [pltpu.VMEM((rows, cols), BF16)],
    )(index, terms)


def fold_kernel(index, near, far, *outs):
    del index
    total = (near[...].astype(F32) + far[...].astype(F32)).astype(BF16)
    rows = outs[0].shape[0]
    for k, out in enumerate(outs):
        out[...] = total[k * rows : (k + 1) * rows, :]


def fold(index, near, far):
    rows, cols = near.shape
    block = (rows // 4, cols)
    return call(
        fold_kernel,
        (1,),
        [whole(near.shape)] * 2,
        [whole(block)] * 4,
        [jax.ShapeDtypeStruct(block, BF16)] * 4,
        8 * rows * cols,
    )(index, near, far)


def body(tokens, gate_weight, up_weight, down_weight, out_grad):
    core = lax.axis_index("row") % NC
    x = (lax.axis_index("row") // NC).astype(jnp.int32).reshape(1)
    col = lax.axis_index("col")
    zyx = jnp.stack([col // NY, col % NY, lax.axis_index("row") // NC]).astype(jnp.int32)
    half = tokens.shape[0] // NC
    width = tokens.shape[1]

    def halves(value):
        mine = lax.dynamic_slice_in_dim(value, core * half, half, 0)
        other = lax.dynamic_slice_in_dim(value, (1 - core) * half, half, 0)
        return mine, swap_core(other)

    def join(value):
        mine = value[:, :width]
        got = swap_core(value[:, width:])
        first = jnp.where(core == 0, mine, got)
        second = jnp.where(core == 0, got, mine)
        return jnp.concatenate([first, second], axis=0)

    tok_a, tok_b = halves(tokens)
    grad_a, grad_b = halves(out_grad)
    own = jnp.concatenate([tok_a, grad_a], axis=1)
    other = jnp.concatenate([tok_b, grad_b], axis=1)
    gate_own, gate_other = in_hbm(gate_weight), in_hbm(swap_core(gate_weight))
    up_own, up_other = in_hbm(up_weight), in_hbm(swap_core(up_weight))
    down_own, down_other = in_hbm(down_weight), in_hbm(swap_core(down_weight))

    other_y = jnp.concatenate(gather_blocks(other, "col", Y_STEP), axis=0)
    other_blocks = ring_eight(other_y, "col", Z_UP, Z_DOWN)
    own_z = share(own, "col", Z_GROUPS)
    own_all = share(after(own_z, other_y), "col", Y_GROUPS)

    gate_up_term, tok_other = gate_up_product(
        zyx, own_all, other_blocks, gate_own, gate_other, up_own, up_other
    )
    gate_up, hidden_own = hidden_of(x, exchange(gate_up_term, "row", X_GROUPS))
    *hidden_terms, grad_other = hidden_term_product(
        zyx, own_all, other_blocks, down_own, down_other
    )
    hidden_terms = [in_hbm(hidden_terms[0])] + [
        lax.ppermute(hidden_terms[k], "row", X_STEP[k]) for k in range(1, NX)
    ]
    pre_own = pre_grads(x, hidden_terms, in_hbm(gate_up))

    hidden_blocks = gather_blocks(hidden_own, "row", X_STEP)
    mixed_term, hidden = mixed_product(after(x, pre_own), hidden_blocks, down_own, down_other)
    pre_blocks = gather_blocks(after(pre_own, *hidden_blocks[1:]), "row", X_STEP)
    input_term, pre_gate, pre_up = input_product(
        after(x, mixed_term), pre_blocks, gate_own, up_own, gate_other, up_other
    )
    mixed_y = exchange(mixed_term, "col", Y_GROUPS)
    input_y = exchange(after(input_term, mixed_y), "col", Y_GROUPS)
    def all_tokens(value):
        return jnp.concatenate([value, swap_core(value)], axis=0)

    tok_rows = jnp.concatenate([own_all[:, :width], swap_core(tok_other)], axis=0)
    grad_rows = jnp.concatenate([own_all[:, width:], swap_core(grad_other)], axis=0)
    down_grad = dot(all_tokens(hidden), grad_rows, TN).astype(BF16)
    gate_grad = dot(tok_rows, all_tokens(pre_gate), TN).astype(BF16)
    input_sum = sum_of(x, after(input_y, down_grad, gate_grad))
    up_grad = dot(tok_rows, after(all_tokens(pre_up), input_sum), TN).astype(BF16)
    near, far = split_sum(zyx, mixed_y)
    previous, mine, following, second = fold(
        zyx, near, after(lax.ppermute(far, "col", Z_STEP[4]), up_grad)
    )
    mixed_sum = mine.astype(F32)
    for block, step in ((previous, NZ - 1), (following, 1), (second, 2)):
        mixed_sum += lax.ppermute(block, "col", Z_STEP[step]).astype(F32)
    mixed = join(mixed_sum.astype(BF16))
    input_sum = after(exchange(input_sum, "col", Z_GROUPS), up_grad, mixed)
    input_grad = join(input_sum.astype(F32).sum(0).astype(BF16))
    return (mixed, input_grad, gate_grad, up_grad, down_grad)


def solution(mesh):
    in_specs = (P("col", "row"), P("row", "col"), P("row", "col"), P("col", "row"), P("col", "row"))
    out_specs = (
        P("col", "row"),
        P("col", "row"),
        P("row", "col"),
        P("row", "col"),
        P("col", "row"),
    )
    return jax.shard_map(body, mesh=mesh, in_specs=in_specs, out_specs=out_specs, check_vma=False)
```

```python
import jax
import jax.numpy as jnp
from jax import lax
from jax.experimental import pallas as pl
from jax.experimental.pallas import tpu as pltpu
from jax.sharding import PartitionSpec as P

BF16 = jnp.bfloat16
F32 = jnp.float32
NX, NC, NZ, NY = 4, 2, 8, 4
MIB = 1024 * 1024
LIMIT = 24
TILE = 256

X_GROUPS = [[x * NC + c for x in range(NX)] for c in range(NC)]
Y_GROUPS = [[z * NY + y for y in range(NY)] for z in range(NZ)]
Z_GROUPS = [[z * NY + y for z in range(NZ)] for y in range(NY)]
Y_STEP = [
    [(z * NY + y, z * NY + (y + k) % NY) for z in range(NZ) for y in range(NY)] for k in range(NY)
]
Z_STEP = [
    [(z * NY + y, (z + k) % NZ * NY + y) for z in range(NZ) for y in range(NY)] for k in range(NZ)
]
Z_UP = [(z * NY + y, (z + 1) % NZ * NY + y) for z in range(NZ) for y in range(NY)]
Z_DOWN = [(dst, src) for src, dst in Z_UP]
X_STEP = [
    [(x * NC + c, (x + k) % NX * NC + c) for x in range(NX) for c in range(NC)] for k in range(NX)
]
CORE_PAIRS = [(r, r ^ 1) for r in range(NX * NC)]

NN = (((1,), (0,)), ((), ()))
NT = (((1,), (1,)), ((), ()))
TN = (((0,), (0,)), ((), ()))


def dot(left, right, dims):
    return lax.dot_general(left, right, dims, preferred_element_type=F32)


def swap_core(value):
    return lax.ppermute(value, "row", CORE_PAIRS)


def exchange(value, axis, groups):
    count = len(groups[0])
    got = lax.all_to_all(value, axis, 0, 0, axis_index_groups=groups, tiled=True)
    return got.reshape(count, value.shape[0] // count, value.shape[1])


def share(value, axis, groups):
    got = exchange(jnp.tile(value, (len(groups[0]), 1)), axis, groups)
    return got.reshape(-1, value.shape[1])


def after(value, *others):
    return lax.optimization_barrier((value,) + others)[0]


def gather_blocks(own, axis, steps):
    count = len(steps)
    return [own] + [lax.ppermute(own, axis, steps[count - k]) for k in range(1, count)]


def ring_eight(own, axis, up, down):
    before, behind = [own], [own]
    for _ in range(4):
        before.append(lax.ppermute(before[-1], axis, up))
    for _ in range(3):
        behind.append(lax.ppermute(behind[-1], axis, down))
    behind[2], before[2] = in_hbm(behind[2]), in_hbm(before[2])
    return own, behind[1], behind[2], behind[3], before[4], before[3], before[2], before[1]


def whole(shape):
    return pl.BlockSpec(shape, lambda *_: (0,) * len(shape))


def hbm(shape, dtype=BF16):
    return pltpu.HBM(shape, dtype)


def in_hbm(value):
    return pltpu.with_memory_space_constraint(value, pltpu.HBM)


def call(kernel, grid, in_specs, out_specs, out_shape, flops, scratch=(), limit=LIMIT):
    return pl.pallas_call(
        kernel,
        grid_spec=pltpu.PrefetchScalarGridSpec(
            num_scalar_prefetch=1,
            grid=grid,
            in_specs=in_specs,
            out_specs=out_specs,
            scratch_shapes=list(scratch),
        ),
        out_shape=out_shape,
        compiler_params=pltpu.CompilerParams(vmem_limit_bytes=limit * MIB),
        cost_estimate=pl.CostEstimate(flops=flops, bytes_accessed=10 * MIB, transcendentals=0),
    )


def place(index, blocks, store):
    rows = blocks[0].shape[0]
    for k, block in enumerate(blocks):
        start = pl.multiple_of(lax.rem(index + k, len(blocks)) * rows, rows)
        store(start, block)


def place_eight(index, blocks, store):
    for step, block in enumerate(blocks):
        z = lax.rem(index[0] + step, NZ)
        for k in range(block.shape[0] // 16):
            y = lax.rem(index[1] + k, NY)
            start = pl.multiple_of(y * NZ * 16 + z * 16, 16)
            store(start, block[k * 16 : (k + 1) * 16, :])


def gate_up_kernel(index, tok_a, *refs):
    blocks, (gate_a, gate_b, up_a, up_b, out, tok_b) = refs[:NZ], refs[NZ:]
    step = pl.program_id(0)

    @pl.when(step == 0)
    def _():
        def store(start, value):
            tok_b[pl.ds(start, 16), :] = value

        place_eight(index, blocks, store)

    tile = gate_a.shape[1]
    gate = dot(tok_a[...], gate_a[...], NN) + dot(tok_b[...], gate_b[...], NN)
    out[:, :tile] = gate.astype(BF16)
    up = dot(tok_a[...], up_a[...], NN) + dot(tok_b[...], up_b[...], NN)
    out[:, tile:] = up.astype(BF16)


def columns(rows, width, at):
    return pl.BlockSpec((rows, width), lambda *_: (0, at))


def gate_up_product(index, own, blocks, gate_a, gate_b, up_a, up_b):
    rows = own.shape[0]
    width, cols = gate_a.shape
    weight = pl.BlockSpec((width, TILE), lambda j, _: (0, j))
    return call(
        gate_up_kernel,
        (cols // TILE,),
        [columns(rows, width, 0)]
        + [columns(block.shape[0], width, 0) for block in blocks]
        + [weight] * 4,
        [pl.BlockSpec((rows, 2 * TILE), lambda j, _: (0, j)), whole((rows, width))],
        [hbm((rows, 2 * cols)), hbm((rows, width))],
        8 * rows * width * cols,
    )(index, own, *blocks, gate_a, gate_b, up_a, up_b)


def hidden_term_kernel(index, grad_a, *refs):
    blocks, (down_a, down_b) = refs[:NZ], refs[NZ : NZ + 2]
    outs, (grad_b, total) = refs[NZ + 2 : NZ + 2 + NX], refs[NZ + 2 + NX :]

    @pl.when(pl.program_id(0) == 0)
    def _():
        def store(start, value):
            grad_b[pl.ds(start, 16), :] = value

        place_eight(index, blocks, store)

    term = dot(grad_a[...], down_a[...], NT) + dot(grad_b[...], down_b[...], NT)
    total[...] = term.astype(BF16)
    rows = outs[0].shape[0]
    for k, out in enumerate(outs):
        start = pl.multiple_of(lax.rem(index[2] + k, NX) * rows, rows)
        out[...] = total[pl.ds(start, rows), :]


def hidden_term_product(index, own, blocks, down_a, down_b):
    rows = own.shape[0]
    cols, width = down_a.shape
    tile = 256
    weight = pl.BlockSpec((tile, width), lambda j, _: (j, 0))
    return call(
        hidden_term_kernel,
        (cols // tile,),
        [columns(rows, width, 1)]
        + [columns(block.shape[0], width, 1) for block in blocks]
        + [weight, weight],
        [pl.BlockSpec((rows // NX, tile), lambda j, _: (0, j))] * NX + [whole((rows, width))],
        [hbm((rows // NX, cols))] * NX + [hbm((rows, width))],
        4 * rows * width * cols,
        [pltpu.VMEM((rows, tile), BF16)],
    )(index, own, *blocks, down_a, down_b)


def mixed_kernel(index, *refs):
    blocks, (down_a, down_b, out, hidden) = refs[:NX], refs[NX:]
    step = pl.program_id(0)

    @pl.when(step == 0)
    def _():
        def store(start, value):
            hidden[pl.ds(start, value.shape[0]), :] = value[...]

        place(index[0], blocks, store)

    tile = down_a.shape[1]
    out[:, :tile] = dot(hidden[...], down_a[...], NN).astype(BF16)
    out[:, tile:] = dot(hidden[...], down_b[...], NN).astype(BF16)


def mixed_product(index, blocks, down_a, down_b):
    rows, depth = blocks[0].shape
    width = down_a.shape[1]
    shape = (4 * rows, depth)
    return call(
        mixed_kernel,
        (width // TILE,),
        [whole(block.shape) for block in blocks]
        + [pl.BlockSpec((depth, TILE), lambda j, _: (0, j))] * 2,
        [pl.BlockSpec((4 * rows, 2 * TILE), lambda j, _: (0, j)), whole(shape)],
        [hbm((4 * rows, 2 * width)), hbm(shape)],
        16 * rows * depth * width,
    )(index, *blocks, down_a, down_b)


def input_kernel(index, *refs):
    blocks, (gate_a, up_a, gate_b, up_b, out, pre_gate, pre_up) = refs[:NX], refs[NX:]
    step = pl.program_id(0)
    cols = blocks[0].shape[1] // 2

    @pl.when(step == 0)
    def _():
        def store(start, value):
            pre_gate[pl.ds(start, value.shape[0]), :] = value[:, :cols]
            pre_up[pl.ds(start, value.shape[0]), :] = value[:, cols:]

        place(index[0], blocks, store)

    tile = gate_a.shape[0]
    mine = dot(pre_gate[...], gate_a[...], NT) + dot(pre_up[...], up_a[...], NT)
    out[:, :tile] = mine.astype(BF16)
    other = dot(pre_gate[...], gate_b[...], NT) + dot(pre_up[...], up_b[...], NT)
    out[:, tile:] = other.astype(BF16)


def input_product(index, blocks, gate_a, up_a, gate_b, up_b):
    rows = blocks[0].shape[0]
    width, cols = gate_a.shape
    weight = pl.BlockSpec((TILE, cols), lambda j, _: (j, 0))
    half = hbm((4 * rows, cols))
    return call(
        input_kernel,
        (width // TILE,),
        [whole(block.shape) for block in blocks] + [weight] * 4,
        [pl.BlockSpec((4 * rows, 2 * TILE), lambda j, _: (0, j))] + [whole((4 * rows, cols))] * 2,
        [hbm((4 * rows, 2 * width)), half, half],
        32 * rows * cols * width,
    )(index, *blocks, gate_a, up_a, gate_b, up_b)


def total_of(terms):
    total = terms[0].astype(F32)
    for k in range(1, terms.shape[0]):
        total = total + terms[k].astype(F32)
    return total


def hidden_kernel(index, terms, gate_up, hidden):
    del index
    total = total_of(terms)
    gate_up[...] = total
    for k in range(hidden.shape[1] // TILE):
        gate = total[:, 2 * k * TILE : (2 * k + 1) * TILE]
        up = total[:, (2 * k + 1) * TILE : (2 * k + 2) * TILE]
        hidden[:, k * TILE : (k + 1) * TILE] = (gate * jax.nn.sigmoid(gate) * up).astype(BF16)


def hidden_of(index, terms):
    _, rows, cols = terms.shape
    return call(
        hidden_kernel,
        (1,),
        [whole(terms.shape)],
        [whole((rows, cols)), whole((rows, cols // 2))],
        [
            hbm((rows, cols), F32),
            jax.ShapeDtypeStruct((rows, cols // 2), BF16),
        ],
        16 * rows * cols,
    )(index, terms)


def pre_kernel(index, *refs):
    del index
    terms, (gate_up, out) = refs[:NX], refs[NX:]
    cols = terms[0].shape[1]
    for k in range(cols // TILE):
        hidden_grad = terms[0][:, k * TILE : (k + 1) * TILE].astype(F32)
        for term in terms[1:]:
            hidden_grad = hidden_grad + term[:, k * TILE : (k + 1) * TILE].astype(F32)
        gate = gate_up[:, 2 * k * TILE : (2 * k + 1) * TILE]
        up = gate_up[:, (2 * k + 1) * TILE : (2 * k + 2) * TILE]
        sig = jax.nn.sigmoid(gate)
        pre_gate = hidden_grad * up * sig * (1.0 + gate * (1.0 - sig))
        out[:, k * TILE : (k + 1) * TILE] = pre_gate.astype(BF16)
        out[:, cols + k * TILE : cols + (k + 1) * TILE] = (hidden_grad * gate * sig).astype(BF16)


def pre_grads(index, terms, gate_up):
    return call(
        pre_kernel,
        (1,),
        [whole(term.shape) for term in terms] + [whole(gate_up.shape)],
        whole(gate_up.shape),
        jax.ShapeDtypeStruct(gate_up.shape, BF16),
        16 * gate_up.size,
    )(index, *terms, gate_up)


def store_sum(terms, out):
    width = out.shape[1] // 2
    for k in range(width // TILE):
        mine = terms[:, :, 2 * k * TILE : (2 * k + 1) * TILE]
        other = terms[:, :, (2 * k + 1) * TILE : (2 * k + 2) * TILE]
        out[:, k * TILE : (k + 1) * TILE] = total_of(mine).astype(BF16)
        out[:, width + k * TILE : width + (k + 1) * TILE] = total_of(other).astype(BF16)


def sum_kernel(index, terms, out):
    del index
    store_sum(terms, out)


def sum_of(index, terms):
    _, rows, cols = terms.shape
    return call(
        sum_kernel,
        (1,),
        [whole(terms.shape)],
        whole((rows, cols)),
        hbm((rows, cols)),
        8 * rows * cols,
    )(index, terms)


def split_kernel(index, terms, near, far, total):
    store_sum(terms, total)
    rows = near.shape[0] // 4
    for k in range(4):
        for step, out in ((k + NZ - 1, near), (k + 3, far)):
            start = pl.multiple_of(lax.rem(index[0] + step, NZ) * rows, 16)
            out[k * rows : (k + 1) * rows, :] = total[pl.ds(start, rows), :]


def split_sum(index, terms):
    _, rows, cols = terms.shape
    half = (rows // 2, cols)
    return call(
        split_kernel,
        (1,),
        [whole(terms.shape)],
        [whole(half)] * 2,
        [jax.ShapeDtypeStruct(half, BF16)] * 2,
        8 * rows * cols,
        [pltpu.VMEM((rows, cols), BF16)],
    )(index, terms)


def fold_kernel(index, near, far, *outs):
    del index
    total = (near[...].astype(F32) + far[...].astype(F32)).astype(BF16)
    rows = outs[0].shape[0]
    for k, out in enumerate(outs):
        out[...] = total[k * rows : (k + 1) * rows, :]


def fold(index, near, far):
    rows, cols = near.shape
    block = (rows // 4, cols)
    return call(
        fold_kernel,
        (1,),
        [whole(near.shape)] * 2,
        [whole(block)] * 4,
        [jax.ShapeDtypeStruct(block, BF16)] * 4,
        8 * rows * cols,
    )(index, near, far)


def body(tokens, gate_weight, up_weight, down_weight, out_grad):
    core = lax.axis_index("row") % NC
    x = (lax.axis_index("row") // NC).astype(jnp.int32).reshape(1)
    col = lax.axis_index("col")
    zyx = jnp.stack([col // NY, col % NY, lax.axis_index("row") // NC]).astype(jnp.int32)
    half = tokens.shape[0] // NC
    width = tokens.shape[1]

    def halves(value):
        mine = lax.dynamic_slice_in_dim(value, core * half, half, 0)
        other = lax.dynamic_slice_in_dim(value, (1 - core) * half, half, 0)
        return mine, swap_core(other)

    def join(value):
        mine = value[:, :width]
        got = swap_core(value[:, width:])
        first = jnp.where(core == 0, mine, got)
        second = jnp.where(core == 0, got, mine)
        return jnp.concatenate([first, second], axis=0)

    tok_a, tok_b = halves(tokens)
    grad_a, grad_b = halves(out_grad)
    own = jnp.concatenate([tok_a, grad_a], axis=1)
    other = jnp.concatenate([tok_b, grad_b], axis=1)
    gate_own, gate_other = in_hbm(gate_weight), in_hbm(swap_core(gate_weight))
    up_own, up_other = in_hbm(up_weight), in_hbm(swap_core(up_weight))
    down_own, down_other = in_hbm(down_weight), in_hbm(swap_core(down_weight))

    other_y = jnp.concatenate(gather_blocks(other, "col", Y_STEP), axis=0)
    other_blocks = ring_eight(other_y, "col", Z_UP, Z_DOWN)
    own_z = share(own, "col", Z_GROUPS)
    own_all = share(after(own_z, other_blocks[7]), "col", Y_GROUPS)

    gate_up_term, tok_other = gate_up_product(
        zyx, own_all, other_blocks, gate_own, gate_other, up_own, up_other
    )
    gate_up, hidden_own = hidden_of(x, exchange(gate_up_term, "row", X_GROUPS))
    *hidden_terms, grad_other = hidden_term_product(
        zyx, own_all, other_blocks, down_own, down_other
    )
    hidden_terms = [in_hbm(hidden_terms[0])] + [
        lax.ppermute(hidden_terms[k], "row", X_STEP[k]) for k in range(1, NX)
    ]
    pre_own = pre_grads(x, hidden_terms, in_hbm(gate_up))

    hidden_blocks = gather_blocks(hidden_own, "row", X_STEP)
    mixed_term, hidden = mixed_product(after(x, pre_own), hidden_blocks, down_own, down_other)
    pre_blocks = gather_blocks(after(pre_own, *hidden_blocks[1:]), "row", X_STEP)
    input_term, pre_gate, pre_up = input_product(
        after(x, mixed_term), pre_blocks, gate_own, up_own, gate_other, up_other
    )
    mixed_y = exchange(mixed_term, "col", Y_GROUPS)
    input_y = exchange(after(input_term, mixed_y), "col", Y_GROUPS)
    def all_tokens(value):
        return jnp.concatenate([value, swap_core(value)], axis=0)

    tok_rows = jnp.concatenate([own_all[:, :width], swap_core(tok_other)], axis=0)
    grad_rows = jnp.concatenate([own_all[:, width:], swap_core(grad_other)], axis=0)
    down_grad = dot(all_tokens(hidden), grad_rows, TN).astype(BF16)
    gate_grad = dot(tok_rows, all_tokens(pre_gate), TN).astype(BF16)
    input_sum = sum_of(x, after(input_y, down_grad, gate_grad))
    up_grad = dot(tok_rows, after(all_tokens(pre_up), input_sum), TN).astype(BF16)
    near, far = split_sum(zyx, mixed_y)
    previous, mine, following, second = fold(
        zyx, near, after(lax.ppermute(far, "col", Z_STEP[4]), up_grad)
    )
    mixed_sum = mine.astype(F32)
    for block, step in ((previous, NZ - 1), (following, 1), (second, 2)):
        mixed_sum += lax.ppermute(block, "col", Z_STEP[step]).astype(F32)
    mixed = join(mixed_sum.astype(BF16))
    input_sum = after(exchange(input_sum, "col", Z_GROUPS), up_grad, mixed)
    input_grad = join(input_sum.astype(F32).sum(0).astype(BF16))
    return (mixed, input_grad, gate_grad, up_grad, down_grad)


def solution(mesh):
    in_specs = (P("col", "row"), P("row", "col"), P("row", "col"), P("col", "row"), P("col", "row"))
    out_specs = (
        P("col", "row"),
        P("col", "row"),
        P("row", "col"),
        P("row", "col"),
        P("col", "row"),
    )
    return jax.shard_map(body, mesh=mesh, in_specs=in_specs, out_specs=out_specs, check_vma=False)
```

```python
import jax
import jax.numpy as jnp
from jax import lax
from jax.experimental import pallas as pl
from jax.experimental.pallas import tpu as pltpu
from jax.sharding import PartitionSpec as P

BF16 = jnp.bfloat16
F32 = jnp.float32
NX, NC, NZ, NY = 4, 2, 8, 4
MIB = 1024 * 1024
LIMIT = 24
TILE = 256

X_GROUPS = [[x * NC + c for x in range(NX)] for c in range(NC)]
Y_GROUPS = [[z * NY + y for y in range(NY)] for z in range(NZ)]
Z_GROUPS = [[z * NY + y for z in range(NZ)] for y in range(NY)]
Y_STEP = [
    [(z * NY + y, z * NY + (y + k) % NY) for z in range(NZ) for y in range(NY)] for k in range(NY)
]
Z_STEP = [
    [(z * NY + y, (z + k) % NZ * NY + y) for z in range(NZ) for y in range(NY)] for k in range(NZ)
]
Z_UP = [(z * NY + y, (z + 1) % NZ * NY + y) for z in range(NZ) for y in range(NY)]
Z_DOWN = [(dst, src) for src, dst in Z_UP]
X_STEP = [
    [(x * NC + c, (x + k) % NX * NC + c) for x in range(NX) for c in range(NC)] for k in range(NX)
]
CORE_PAIRS = [(r, r ^ 1) for r in range(NX * NC)]

NN = (((1,), (0,)), ((), ()))
NT = (((1,), (1,)), ((), ()))
TN = (((0,), (0,)), ((), ()))


def dot(left, right, dims):
    return lax.dot_general(left, right, dims, preferred_element_type=F32)


def swap_core(value):
    return lax.ppermute(value, "row", CORE_PAIRS)


def exchange(value, axis, groups):
    count = len(groups[0])
    got = lax.all_to_all(value, axis, 0, 0, axis_index_groups=groups, tiled=True)
    return got.reshape(count, value.shape[0] // count, value.shape[1])


def share(value, axis, groups):
    got = exchange(jnp.tile(value, (len(groups[0]), 1)), axis, groups)
    return got.reshape(-1, value.shape[1])


def after(value, *others):
    return lax.optimization_barrier((value,) + others)[0]


def gather_blocks(own, axis, steps):
    count = len(steps)
    return [own] + [lax.ppermute(own, axis, steps[count - k]) for k in range(1, count)]


def ring_eight(own, axis, up, down):
    before, behind = [own], [own]
    for _ in range(4):
        before.append(lax.ppermute(before[-1], axis, up))
    for _ in range(3):
        behind.append(lax.ppermute(behind[-1], axis, down))
    behind[2], before[2] = in_hbm(behind[2]), in_hbm(before[2])
    return own, behind[1], behind[2], behind[3], before[4], before[3], before[2], before[1]


def whole(shape):
    return pl.BlockSpec(shape, lambda *_: (0,) * len(shape))


def hbm(shape, dtype=BF16):
    return pltpu.HBM(shape, dtype)


def in_hbm(value):
    return pltpu.with_memory_space_constraint(value, pltpu.HBM)


def call(kernel, grid, in_specs, out_specs, out_shape, flops, scratch=(), limit=LIMIT):
    return pl.pallas_call(
        kernel,
        grid_spec=pltpu.PrefetchScalarGridSpec(
            num_scalar_prefetch=1,
            grid=grid,
            in_specs=in_specs,
            out_specs=out_specs,
            scratch_shapes=list(scratch),
        ),
        out_shape=out_shape,
        compiler_params=pltpu.CompilerParams(vmem_limit_bytes=limit * MIB),
        cost_estimate=pl.CostEstimate(flops=flops, bytes_accessed=10 * MIB, transcendentals=0),
    )


def place(index, blocks, store):
    rows = blocks[0].shape[0]
    for k, block in enumerate(blocks):
        start = pl.multiple_of(lax.rem(index + k, len(blocks)) * rows, rows)
        store(start, block)


def place_eight(index, blocks, store):
    for step, block in enumerate(blocks):
        z = lax.rem(index[0] + step, NZ)
        for k in range(block.shape[0] // 16):
            y = lax.rem(index[1] + k, NY)
            start = pl.multiple_of(y * NZ * 16 + z * 16, 16)
            store(start, block[k * 16 : (k + 1) * 16, :])


def gate_up_kernel(index, tok_a, *refs):
    blocks, (gate_a, gate_b, up_a, up_b, out, tok_b) = refs[:NZ], refs[NZ:]
    step = pl.program_id(0)

    @pl.when(step == 0)
    def _():
        def store(start, value):
            tok_b[pl.ds(start, 16), :] = value

        place_eight(index, blocks, store)

    tile = gate_a.shape[1]
    gate = dot(tok_a[...], gate_a[...], NN) + dot(tok_b[...], gate_b[...], NN)
    out[:, :tile] = gate.astype(BF16)
    up = dot(tok_a[...], up_a[...], NN) + dot(tok_b[...], up_b[...], NN)
    out[:, tile:] = up.astype(BF16)


def columns(rows, width, at):
    return pl.BlockSpec((rows, width), lambda *_: (0, at))


def gate_up_product(index, own, blocks, gate_a, gate_b, up_a, up_b):
    rows = own.shape[0]
    width, cols = gate_a.shape
    weight = pl.BlockSpec((width, TILE), lambda j, _: (0, j))
    return call(
        gate_up_kernel,
        (cols // TILE,),
        [columns(rows, width, 0)]
        + [columns(block.shape[0], width, 0) for block in blocks]
        + [weight] * 4,
        [pl.BlockSpec((rows, 2 * TILE), lambda j, _: (0, j)), whole((rows, width))],
        [hbm((rows, 2 * cols)), hbm((rows, width))],
        8 * rows * width * cols,
    )(index, own, *blocks, gate_a, gate_b, up_a, up_b)


def hidden_term_kernel(index, grad_a, *refs):
    blocks, (down_a, down_b) = refs[:NZ], refs[NZ : NZ + 2]
    outs, (grad_b, total) = refs[NZ + 2 : NZ + 2 + NX], refs[NZ + 2 + NX :]

    @pl.when(pl.program_id(0) == 0)
    def _():
        def store(start, value):
            grad_b[pl.ds(start, 16), :] = value

        place_eight(index, blocks, store)

    term = dot(grad_a[...], down_a[...], NT) + dot(grad_b[...], down_b[...], NT)
    total[...] = term.astype(BF16)
    rows = outs[0].shape[0]
    for k, out in enumerate(outs):
        start = pl.multiple_of(lax.rem(index[2] + k, NX) * rows, rows)
        out[...] = total[pl.ds(start, rows), :]


def hidden_term_product(index, own, blocks, down_a, down_b):
    rows = own.shape[0]
    cols, width = down_a.shape
    tile = 256
    weight = pl.BlockSpec((tile, width), lambda j, _: (j, 0))
    return call(
        hidden_term_kernel,
        (cols // tile,),
        [columns(rows, width, 1)]
        + [columns(block.shape[0], width, 1) for block in blocks]
        + [weight, weight],
        [pl.BlockSpec((rows // NX, tile), lambda j, _: (0, j))] * NX + [whole((rows, width))],
        [hbm((rows // NX, cols))] * NX + [hbm((rows, width))],
        4 * rows * width * cols,
        [pltpu.VMEM((rows, tile), BF16)],
    )(index, own, *blocks, down_a, down_b)


def mixed_kernel(index, *refs):
    blocks, (down_a, down_b, out, hidden) = refs[:NX], refs[NX:]
    step = pl.program_id(0)

    @pl.when(step == 0)
    def _():
        def store(start, value):
            hidden[pl.ds(start, value.shape[0]), :] = value[...]

        place(index[0], blocks, store)

    tile = down_a.shape[1]
    out[:, :tile] = dot(hidden[...], down_a[...], NN).astype(BF16)
    out[:, tile:] = dot(hidden[...], down_b[...], NN).astype(BF16)


def mixed_product(index, blocks, down_a, down_b):
    rows, depth = blocks[0].shape
    width = down_a.shape[1]
    shape = (4 * rows, depth)
    return call(
        mixed_kernel,
        (width // TILE,),
        [whole(block.shape) for block in blocks]
        + [pl.BlockSpec((depth, TILE), lambda j, _: (0, j))] * 2,
        [pl.BlockSpec((4 * rows, 2 * TILE), lambda j, _: (0, j)), whole(shape)],
        [hbm((4 * rows, 2 * width)), hbm(shape)],
        16 * rows * depth * width,
    )(index, *blocks, down_a, down_b)


def input_kernel(index, *refs):
    blocks, (gate_a, up_a, gate_b, up_b, out, pre_gate, pre_up) = refs[:NX], refs[NX:]
    step = pl.program_id(0)
    cols = blocks[0].shape[1] // 2

    @pl.when(step == 0)
    def _():
        def store(start, value):
            pre_gate[pl.ds(start, value.shape[0]), :] = value[:, :cols]
            pre_up[pl.ds(start, value.shape[0]), :] = value[:, cols:]

        place(index[0], blocks, store)

    tile = gate_a.shape[0]
    mine = dot(pre_gate[...], gate_a[...], NT) + dot(pre_up[...], up_a[...], NT)
    out[:, :tile] = mine.astype(BF16)
    other = dot(pre_gate[...], gate_b[...], NT) + dot(pre_up[...], up_b[...], NT)
    out[:, tile:] = other.astype(BF16)


def input_product(index, blocks, gate_a, up_a, gate_b, up_b):
    rows = blocks[0].shape[0]
    width, cols = gate_a.shape
    weight = pl.BlockSpec((TILE, cols), lambda j, _: (j, 0))
    half = hbm((4 * rows, cols))
    return call(
        input_kernel,
        (width // TILE,),
        [whole(block.shape) for block in blocks] + [weight] * 4,
        [pl.BlockSpec((4 * rows, 2 * TILE), lambda j, _: (0, j))] + [whole((4 * rows, cols))] * 2,
        [hbm((4 * rows, 2 * width)), half, half],
        32 * rows * cols * width,
    )(index, *blocks, gate_a, up_a, gate_b, up_b)


def total_of(terms):
    total = terms[0].astype(F32)
    for k in range(1, terms.shape[0]):
        total = total + terms[k].astype(F32)
    return total


def hidden_kernel(index, terms, gate_up, hidden):
    del index
    total = total_of(terms)
    gate_up[...] = total
    for k in range(hidden.shape[1] // TILE):
        gate = total[:, 2 * k * TILE : (2 * k + 1) * TILE]
        up = total[:, (2 * k + 1) * TILE : (2 * k + 2) * TILE]
        hidden[:, k * TILE : (k + 1) * TILE] = (gate * jax.nn.sigmoid(gate) * up).astype(BF16)


def hidden_of(index, terms):
    _, rows, cols = terms.shape
    return call(
        hidden_kernel,
        (1,),
        [whole(terms.shape)],
        [whole((rows, cols)), whole((rows, cols // 2))],
        [
            hbm((rows, cols), F32),
            jax.ShapeDtypeStruct((rows, cols // 2), BF16),
        ],
        16 * rows * cols,
    )(index, terms)


def pre_kernel(index, *refs):
    del index
    terms, (gate_up, out) = refs[:NX], refs[NX:]
    cols = terms[0].shape[1]
    for k in range(cols // TILE):
        hidden_grad = terms[0][:, k * TILE : (k + 1) * TILE].astype(F32)
        for term in terms[1:]:
            hidden_grad = hidden_grad + term[:, k * TILE : (k + 1) * TILE].astype(F32)
        gate = gate_up[:, 2 * k * TILE : (2 * k + 1) * TILE]
        up = gate_up[:, (2 * k + 1) * TILE : (2 * k + 2) * TILE]
        sig = jax.nn.sigmoid(gate)
        pre_gate = hidden_grad * up * sig * (1.0 + gate * (1.0 - sig))
        out[:, k * TILE : (k + 1) * TILE] = pre_gate.astype(BF16)
        out[:, cols + k * TILE : cols + (k + 1) * TILE] = (hidden_grad * gate * sig).astype(BF16)


def pre_grads(index, terms, gate_up):
    return call(
        pre_kernel,
        (1,),
        [whole(term.shape) for term in terms] + [whole(gate_up.shape)],
        whole(gate_up.shape),
        jax.ShapeDtypeStruct(gate_up.shape, BF16),
        16 * gate_up.size,
    )(index, *terms, gate_up)


def store_sum(terms, out):
    width = out.shape[1] // 2
    for k in range(width // TILE):
        mine = terms[:, :, 2 * k * TILE : (2 * k + 1) * TILE]
        other = terms[:, :, (2 * k + 1) * TILE : (2 * k + 2) * TILE]
        out[:, k * TILE : (k + 1) * TILE] = total_of(mine).astype(BF16)
        out[:, width + k * TILE : width + (k + 1) * TILE] = total_of(other).astype(BF16)


def sum_kernel(index, terms, out):
    del index
    store_sum(terms, out)


def sum_of(index, terms):
    _, rows, cols = terms.shape
    return call(
        sum_kernel,
        (1,),
        [whole(terms.shape)],
        whole((rows, cols)),
        hbm((rows, cols)),
        8 * rows * cols,
    )(index, terms)


def split_kernel(index, terms, near, far, total):
    store_sum(terms, total)
    rows = near.shape[0] // 4
    for k in range(4):
        for step, out in ((k + NZ - 1, near), (k + 3, far)):
            start = pl.multiple_of(lax.rem(index[0] + step, NZ) * rows, 16)
            out[k * rows : (k + 1) * rows, :] = total[pl.ds(start, rows), :]


def split_sum(index, terms):
    _, rows, cols = terms.shape
    half = (rows // 2, cols)
    return call(
        split_kernel,
        (1,),
        [whole(terms.shape)],
        [whole(half)] * 2,
        [jax.ShapeDtypeStruct(half, BF16)] * 2,
        8 * rows * cols,
        [pltpu.VMEM((rows, cols), BF16)],
    )(index, terms)


def fold_kernel(index, near, far, *outs):
    del index
    total = (near[...].astype(F32) + far[...].astype(F32)).astype(BF16)
    rows = outs[0].shape[0]
    for k, out in enumerate(outs):
        out[...] = total[k * rows : (k + 1) * rows, :]


def fold(index, near, far):
    rows, cols = near.shape
    block = (rows // 4, cols)
    return call(
        fold_kernel,
        (1,),
        [whole(near.shape)] * 2,
        [whole(block)] * 4,
        [jax.ShapeDtypeStruct(block, BF16)] * 4,
        8 * rows * cols,
    )(index, near, far)


def body(tokens, gate_weight, up_weight, down_weight, out_grad):
    core = lax.axis_index("row") % NC
    x = (lax.axis_index("row") // NC).astype(jnp.int32).reshape(1)
    col = lax.axis_index("col")
    zyx = jnp.stack([col // NY, col % NY, lax.axis_index("row") // NC]).astype(jnp.int32)
    half = tokens.shape[0] // NC
    width = tokens.shape[1]

    def halves(value):
        mine = lax.dynamic_slice_in_dim(value, core * half, half, 0)
        other = lax.dynamic_slice_in_dim(value, (1 - core) * half, half, 0)
        return mine, swap_core(other)

    def join(value):
        mine = value[:, :width]
        got = swap_core(value[:, width:])
        first = jnp.where(core == 0, mine, got)
        second = jnp.where(core == 0, got, mine)
        return jnp.concatenate([first, second], axis=0)

    tok_a, tok_b = halves(tokens)
    grad_a, grad_b = halves(out_grad)
    own = jnp.concatenate([tok_a, grad_a], axis=1)
    other = jnp.concatenate([tok_b, grad_b], axis=1)
    gate_own, gate_other = in_hbm(gate_weight), in_hbm(swap_core(gate_weight))
    up_own, up_other = in_hbm(up_weight), in_hbm(swap_core(up_weight))
    down_own, down_other = in_hbm(down_weight), in_hbm(swap_core(down_weight))

    other_y = jnp.concatenate(gather_blocks(other, "col", Y_STEP), axis=0)
    other_blocks = ring_eight(other_y, "col", Z_UP, Z_DOWN)
    own_z = share(own, "col", Z_GROUPS)
    own_all = share(after(own_z, other_y), "col", Y_GROUPS)

    gate_up_term, tok_other = gate_up_product(
        zyx, own_all, other_blocks, gate_own, gate_other, up_own, up_other
    )
    gate_up, hidden_own = hidden_of(x, exchange(gate_up_term, "row", X_GROUPS))
    *hidden_terms, grad_other = hidden_term_product(
        zyx, own_all, other_blocks, down_own, down_other
    )
    hidden_terms = [in_hbm(hidden_terms[0])] + [
        lax.ppermute(hidden_terms[k], "row", X_STEP[k]) for k in range(1, NX)
    ]
    pre_own = pre_grads(x, hidden_terms, in_hbm(gate_up))

    hidden_blocks = gather_blocks(hidden_own, "row", X_STEP)
    mixed_term, hidden = mixed_product(after(x, pre_own), hidden_blocks, down_own, down_other)
    pre_blocks = gather_blocks(after(pre_own, *hidden_blocks[1:]), "row", X_STEP)
    input_term, pre_gate, pre_up = input_product(
        after(x, mixed_term), pre_blocks, gate_own, up_own, gate_other, up_other
    )
    mixed_y = exchange(mixed_term, "col", Y_GROUPS)
    input_y = exchange(after(input_term, mixed_y), "col", Y_GROUPS)
    def all_tokens(value):
        return jnp.concatenate([value, swap_core(value)], axis=0)

    tok_rows = jnp.concatenate([own_all[:, :width], swap_core(tok_other)], axis=0)
    grad_rows = jnp.concatenate([own_all[:, width:], swap_core(grad_other)], axis=0)
    down_grad = dot(all_tokens(hidden), grad_rows, TN).astype(BF16)
    gate_grad = dot(tok_rows, all_tokens(pre_gate), TN).astype(BF16)
    input_sum = sum_of(x, after(input_y, down_grad, gate_grad))
    up_grad = dot(tok_rows, after(all_tokens(pre_up), input_sum), TN).astype(BF16)
    near, far = split_sum(zyx, mixed_y)
    previous, mine, following, second = fold(
        zyx, near, after(lax.ppermute(far, "col", Z_STEP[4]), up_grad)
    )
    mixed_sum = mine.astype(F32)
    for block, step in ((previous, NZ - 1), (following, 1), (second, 2)):
        mixed_sum += lax.ppermute(block, "col", Z_STEP[step]).astype(F32)
    mixed = join(mixed_sum.astype(BF16))
    input_sum = after(exchange(input_sum, "col", Z_GROUPS), up_grad, mixed)
    input_grad = join(input_sum.astype(F32).sum(0).astype(BF16))
    return (mixed, input_grad, gate_grad, up_grad, down_grad)


def solution(mesh):
    in_specs = (P("col", "row"), P("row", "col"), P("row", "col"), P("col", "row"), P("col", "row"))
    out_specs = (
        P("col", "row"),
        P("col", "row"),
        P("row", "col"),
        P("row", "col"),
        P("col", "row"),
    )
    return jax.shard_map(body, mesh=mesh, in_specs=in_specs, out_specs=out_specs, check_vma=False)
```
